512 devices in a mesh: ha: 16 (over y, core), wa: 32 (over z, x).
Axes of the slice: x: 4, y: 8, z: 8, core: 2. Of those that a mesh axis runs over, the one named last changes fastest.
Arguments:
- volume: bfloat16 [4, 64, 256, 32], P(None, 'ha', 'wa'), may hold values from -6 to 6
- hidden_pre: bfloat16 [128, 64, 256, 32], P(None, 'ha', 'wa'), may hold values from -6 to 6
- grad_out: bfloat16 [128, 64, 256, 32], P(None, 'ha', 'wa'), may hold values from -0.008239746 to 0.008239746
- weight_two: bfloat16 [3, 3, 3, 128, 128], replicated, may hold values from -0.109375 to 0.109375
Outputs:
- grad_one: float32 [3, 3, 3, 4, 128], replicated
- grad_two: float32 [3, 3, 3, 128, 128], replicated
The draws below stay inside these ranges and needn't reach their ends.
All inputs are finite; a program needn't handle non-finite values.
Results may differ from the reference program's by a relative error of at most 0.0034.
Values may be sent and summed in bfloat16 or wider, within the bound.
A program may use at most 64 MiB of HBM per device.

```python
import jax
import jax.numpy as jnp
from jax import lax

C_IN = 4
CH = 128
DEP = 32
NH = 64
NW = 256


def levels(own_key, extent, split, smallest, top_value):
    loudness, own = 1.0, jax.random.fold_in(own_key, 6)
    for position, parts in split:
        draws = jnp.exp(jax.random.uniform(jax.random.fold_in(own, position), (parts,), jnp.float32, smallest / len(split), top_value / len(split)))
        loudness = loudness * jnp.repeat(draws, extent[position] // parts).reshape([-1 if axis == position else 1 for axis in range(len(extent))])
    return loudness


def normal_values(key, shape, deviation, bound, pieces=(), kind=jnp.bfloat16):
    entries = deviation * jax.random.normal(key, shape, jnp.float32)
    if pieces:
        entries = entries * levels(key, shape, pieces, -0.22, 0.18)
    return jnp.clip(entries, -bound, bound).astype(kind)


def setup_inputs(seed: int = 0) -> dict:
    seeds = jax.random.split(jax.random.key(seed), 5)
    return {
        "volume": normal_values(seeds[0], (C_IN, NH, NW, DEP), 1.0, 6.0, ((1, 16), (2, 32))),
        "hidden_pre": normal_values(seeds[1], (CH, NH, NW, DEP), 1.0, 6.0, ((1, 16), (2, 32))),
        "grad_out": normal_values(seeds[2], (CH, NH, NW, DEP), (1.0 / (NH * NW * DEP) ** 0.5), 0.008239746, ((1, 16), (2, 32))),
        "weight_two": normal_values(seeds[3], (3, 3, 3, CH, CH), (27 * CH) ** -0.5, 0.109375),
    }


def convolve(field, kernel):
    result = lax.conv_general_dilated(field[None], kernel, (1, 1, 1), ((1, 1), (1, 1), (1, 1)), dimension_numbers=('NCHWD', 'HWDIO', 'NCHWD'), precision=lax.Precision.HIGHEST)
    return result[0]

def reference(volume, hidden_pre, grad_out, weight_two):
    active = jnp.maximum(hidden_pre, 0).astype(jnp.float32)
    grad_wide = grad_out.astype(jnp.float32)
    unused, pull_two = jax.vjp(convolve, active, weight_two.astype(jnp.float32))
    grad_act, grad_two = pull_two(grad_wide)
    grad_hidden = (grad_act * (hidden_pre > 0).astype(jnp.float32)).astype(jnp.bfloat16)
    volume_wide = volume.astype(jnp.float32)
    kernel_zero = jnp.zeros((3, 3, 3, C_IN, CH), jnp.float32)
    unused_one, pull_one = jax.vjp(lambda kernel: convolve(volume_wide, kernel), kernel_zero)
    grad_one = pull_one(grad_hidden.astype(jnp.float32))[0]
    return (grad_one, grad_two)
```

```python
import functools

import jax
import jax.numpy as jnp
from jax import lax
from jax.experimental import pallas as pl
from jax.experimental.pallas import tpu as pltpu
from jax.sharding import PartitionSpec as P

MESH = pl.DeviceIdType.MESH
F32 = jnp.float32
BF16 = jnp.bfloat16
NY, NZ, NX = 8, 8, 4
TAPS = 28
GROUPS = 7
SIDES = [(a, b) for a in (-1, 0, 1) for b in (-1, 0, 1) if (a, b) != (0, 0)]
X_STEPS = (1, 3, 2)
RING = (1, 7, 2, 6, 3, 5, 4)


def span(side, size):
    if side == 0:
        return slice(0, size), slice(1, size + 1)
    if side == 1:
        return slice(size - 1, size), slice(0, 1)
    return slice(0, 1), slice(size + 1, size + 2)


def kernel(
    vol_ref, hid_ref, go_ref, w_ref, out_ref,
    ext, vols, hid, w, act_t, part, core_rx, x_tx, x_rx, y_tx, y_rx, y_own, z_all,
    load_sem, halo_ss, halo_rs, core_ss, core_rs, x_ss, x_rs, y_ss, y_rs, z_ss, z_rs,
    yg_ss, yg_rs, xg_ss, xg_rs, cg_ss, cg_rs,
):
    ha = lax.axis_index("ha")
    wa = lax.axis_index("wa")
    ys, core = ha // 2, ha % 2
    zs, xs = wa // 4, wa % 4
    n_ha, n_wa = 2 * NY, NX * NZ

    def dev(y, c, z, x):
        return (y * 2 + c, z * NX + x)

    def near(side):
        return ((ha + side[0] + n_ha) % n_ha, (wa + side[1] + n_wa) % n_wa)

    other = dev(ys, 1 - core, zs, xs)
    x_peer = [dev(ys, core, zs, (xs + i) % NX) for i in X_STEPS]
    y_peer = [dev((ys + i) % NY, core, zs, xs) for i in RING]
    z_peer = [dev(ys, core, (zs + i) % NZ, xs) for i in RING]

    loads = [
        pltpu.make_async_copy(hid_ref, hid, load_sem.at[0]),
        pltpu.make_async_copy(go_ref, ext.at[1:5, 1:9], load_sem.at[1]),
        pltpu.make_async_copy(vol_ref, vols.at[4], load_sem.at[2]),
        pltpu.make_async_copy(w_ref, w, load_sem.at[3]),
    ]
    for c in loads:
        c.start()

    barrier = pltpu.get_barrier_semaphore()
    greet = [near(s) for s in SIDES] + x_peer + y_peer + z_peer
    for d in greet:
        pl.semaphore_signal(barrier, inc=1, device_id=d, device_id_type=MESH)

    copies = []

    def send(src, dst, ss, rs, device):
        c = pltpu.make_async_remote_copy(
            src_ref=src, dst_ref=dst, send_sem=ss, recv_sem=rs,
            device_id=device, device_id_type=MESH,
        )
        return c

    halo = []
    for n, side in enumerate(SIDES):
        (sh, dh), (sw, dw) = span(side[0], 4), span(side[1], 8)
        slot = (1 - side[0]) * 3 + (1 - side[1])
        halo.append(send(go_ref.at[sh, sw], ext.at[dh, dw], halo_ss.at[n], halo_rs.at[n], near(side)))
        halo.append(send(vol_ref, vols.at[slot], halo_ss.at[8 + n], halo_rs.at[8 + n], near(side)))

    pl.semaphore_wait(barrier, len(greet))
    for c in halo[0::2] + halo[1::2]:
        c.start()

    loads[0].wait()
    depth = lax.broadcasted_iota(jnp.int32, (1024, 128), 0) % 32
    act = jnp.maximum(hid[...], 0).astype(F32).reshape(1024, 128)
    act_t[128:256, :] = act.astype(BF16).T
    lower = jnp.where(depth == 0, 0.0, pltpu.roll(act, 1, 0))
    act_t[0:128, :] = lower.astype(BF16).T
    upper = jnp.where(depth == 31, 0.0, pltpu.roll(act, 1023, 0))
    act_t[256:384, :] = upper.astype(BF16).T

    for c in loads[1:]:
        c.wait()
    for c in halo:
        c.wait()

    for edge, rows in ((0, slice(0, 1)), (n_ha - 1, slice(5, 6))):
        @pl.when(ha == edge)
        def _(rows=rows):
            ext[rows] = jnp.zeros((1, 10, 32, 128), BF16)
            first = 0 if rows.start == 0 else 6
            vols[first : first + 3] = jnp.zeros((3, 32, 256), BF16)

    for edge, cols in ((0, slice(0, 1)), (n_wa - 1, slice(9, 10))):
        @pl.when(wa == edge)
        def _(cols=cols):
            ext[:, cols] = jnp.zeros((6, 1, 32, 128), BF16)
            first = 0 if cols.start == 0 else 2
            for n in (first, first + 3, first + 6):
                vols[n] = jnp.zeros((32, 256), BF16)

    def window(g):
        kh, kw = g // 3, g % 3
        return ext[2 - kh : 6 - kh, 2 - kw : 10 - kw].reshape(1024, 128)

    def taps_of(g):
        return slice(3 * g, 3 * g + 3) if g < 9 else slice(27, 28)

    their_half = pl.ds(pl.multiple_of((1 - core) * 64, 64), 64)
    own_half = pl.ds(pl.multiple_of(core * 64, 64), 64)
    own_in_half = pl.ds(pl.multiple_of(xs * 16, 16), 16)
    own_rows = pl.ds(pl.multiple_of(core * 64 + xs * 16, 16), 16)

    def rows_of(c, x):
        return pl.ds(pl.multiple_of(c * 64 + x * 16, 16), 16)

    core_copies = []

    def core_send(g):
        t = taps_of(g)
        c = send(part.at[t, their_half], core_rx.at[t], core_ss.at[g], core_rs.at[g], other)
        c.start()
        core_copies.append(c)

    x_copies = []

    def x_send(g):
        t = taps_of(g)
        core_copies[g].wait_recv()
        x_tx[t] = (part[t, own_half] + core_rx[t]).astype(BF16)
        row = []
        for i, step in enumerate(X_STEPS):
            rows = pl.ds(pl.multiple_of((xs + step) % NX * 16, 16), 16)
            c = send(x_tx.at[t, rows], x_rx.at[i, t], x_ss.at[g, i], x_rs.at[g, i], x_peer[i])
            c.start()
            row.append(c)
        x_copies.append(row)

    for pair in ((0, 1), (2, 3), (4, 5), (6, 7), (8,)):
        right = jnp.concatenate([window(g) for g in pair], axis=1)
        terms = jnp.dot(act_t[...], right, preferred_element_type=F32)
        for n, g in enumerate(pair):
            part[taps_of(g)] = terms[:, 128 * n : 128 * n + 128].reshape(3, 128, 128)
            core_send(g)
        for g in pair:
            if g >= 2:
                x_send(g - 2)

    def column(n):
        return jnp.concatenate(
            [vols[n, 24:32], vols[3 + n], vols[6 + n, 0:8]], axis=0
        ).astype(F32)

    left, centre, right = column(0), column(1), column(2)
    lane = lax.broadcasted_iota(jnp.int32, (48, 256), 1)
    by_w = [
        jnp.where(lane < 32, pltpu.roll(left, 32, 1), pltpu.roll(centre, 32, 1)),
        centre,
        jnp.where(lane >= 224, pltpu.roll(right, 224, 1), pltpu.roll(centre, 224, 1)),
    ]
    blocks = []
    for field in by_w:
        blocks.append(jnp.where(lane % 32 == 0, 0.0, pltpu.roll(field, 1, 1)))
        blocks.append(field)
        blocks.append(jnp.where(lane % 32 == 31, 0.0, pltpu.roll(field, 255, 1)))
    fields = jnp.concatenate(blocks, axis=0).astype(BF16)

    one = [[jnp.zeros((8, 128), F32) for _ in range(3)] for _ in range(9)]
    depth_row = lax.broadcasted_iota(jnp.int32, (256, 128), 0) % 32
    weights = jnp.concatenate([w[g] for g in range(9)], axis=1)
    for h in range(4):
        cells = jnp.concatenate(
            [
                ext[h + 2 - g // 3, 2 - g % 3 : 10 - g % 3].reshape(256, 128)
                for g in range(9)
            ],
            axis=1,
        )
        pulled = lax.dot_general(
            cells, weights, (((1,), (1,)), ((), ())), preferred_element_type=F32
        )
        grad = (
            jnp.where(depth_row == 31, 0.0, pltpu.roll(pulled[:, 0:128], 255, 0))
            + pulled[:, 128:256]
            + jnp.where(depth_row == 0, 0.0, pltpu.roll(pulled[:, 256:384], 1, 0))
        )
        mask = hid[h].reshape(256, 128).astype(F32) > 0
        grad_hidden = jnp.where(mask, grad, 0.0).astype(BF16)
        terms = jnp.dot(fields, grad_hidden, preferred_element_type=F32)
        for b in range(9):
            for kh in range(3):
                first = b * 48 + (h + kh) * 8
                one[b][kh] = one[b][kh] + terms[first : first + 8]
        if h == 1:
            x_send(7)
            x_send(8)
    part[27] = jnp.zeros((128, 128), F32)
    for b in range(9):
        for kh in range(3):
            first = (b * 3 + kh) * 4
            part[27, first : first + 4, :] = one[b][kh][0:4]
    core_send(9)

    def group(j):
        return slice(4 * j, 4 * j + 4)

    def y_copy(j):
        return send(
            y_tx.at[j], y_rx.at[ys], y_ss.at[j], y_rs.at[ys], dev(j, core, zs, xs)
        )

    y_rx[ys] = jnp.zeros((4, 16, 128), BF16)
    waited = 0
    for j in range(GROUPS):
        if j == GROUPS - 1:
            x_send(9)
        need = 10 if j == GROUPS - 1 else (4 * j + 3) // 3 + 1
        while waited < need:
            for c in x_copies[waited]:
                c.wait_recv()
            waited += 1
        t = group(j)
        total = part[t, own_rows] + core_rx[t, own_in_half]
        for i in range(3):
            total = total + x_rx[i, t].astype(F32)

        @pl.when(ys == j)
        def _(total=total):
            y_own[...] = total

        @pl.when(ys != j)
        def _(total=total, j=j):
            y_tx[j] = total.astype(BF16)
            y_copy(j).start()

    own_group = pl.ds(ys * 4, 4)

    def z_copy(i):
        return send(z_all.at[zs], z_all.at[zs], z_ss.at[i], z_rs.at[i], z_peer[i])

    def yg_copy(i):
        place = out_ref.at[own_group, own_rows]
        return send(place, place, yg_ss.at[i], yg_rs.at[ys], y_peer[i])

    @pl.when(ys < GROUPS)
    def _():
        for s in range(NY):
            @pl.when(ys != s)
            def _(s=s):
                send(y_tx.at[0], y_rx.at[s], y_ss.at[0], y_rs.at[s], other).wait_recv()

        total = y_own[...]
        for s in range(NY):
            total = total + y_rx[s].astype(F32)
        z_all[zs] = total
        for i in range(7):
            z_copy(i).start()
        for i in range(7):
            z_copy(i).wait_recv()
        total = z_all[0]
        for s in range(1, NZ):
            total = total + z_all[s]
        out_ref[own_group, own_rows] = total.astype(BF16)
        for i in range(7):
            yg_copy(i).start()

    def xg_copy(j, i):
        place = out_ref.at[group(j), own_rows]
        return send(place, place, xg_ss.at[j, i], xg_rs.at[j, i], x_peer[i])

    def cg_copy(j, i):
        x = xs if i == 3 else (xs + NX - X_STEPS[i]) % NX
        place = out_ref.at[group(j), rows_of(core, x)]
        return send(place, place, cg_ss.at[j, i], cg_rs.at[j, i], other)

    for j in range(GROUPS):
        @pl.when(ys != j)
        def _(j=j):
            place = out_ref.at[group(j), own_rows]
            send(place, place, yg_ss.at[0], yg_rs.at[j], other).wait_recv()

        for i in range(3):
            xg_copy(j, i).start()
        cg_copy(j, 3).start()
    for j in range(GROUPS):
        for i in range(3):
            xg_copy(j, i).wait_recv()
            cg_copy(j, i).start()
    for j in range(GROUPS):
        for i in range(4):
            cg_copy(j, i).wait_recv()

    for c in core_copies:
        c.wait_send()
    for row in x_copies:
        for c in row:
            c.wait_send()
    for j in range(GROUPS):
        @pl.when(ys != j)
        def _(j=j):
            y_copy(j).wait_send()

    @pl.when(ys < GROUPS)
    def _():
        for i in range(7):
            z_copy(i).wait_send()
        for i in range(7):
            yg_copy(i).wait_send()

    for j in range(GROUPS):
        for i in range(3):
            xg_copy(j, i).wait_send()
        for i in range(4):
            cg_copy(j, i).wait_send()


def body(volume, hidden_pre, grad_out, weight_two):
    vol = jnp.transpose(volume, (1, 0, 2, 3)).reshape(4, 4, 256)
    vol = jnp.pad(vol, ((0, 0), (0, 4), (0, 0))).reshape(32, 256)
    hid = jnp.transpose(hidden_pre, (1, 2, 3, 0))
    grad = jnp.transpose(grad_out, (1, 2, 3, 0))
    weights = weight_two.reshape(9, 384, 128)
    dma = pltpu.SemaphoreType.DMA
    out = pl.pallas_call(
        kernel,
        out_shape=jax.ShapeDtypeStruct((TAPS, 128, 128), BF16),
        in_specs=[pl.BlockSpec(memory_space=pl.ANY)] * 4,
        out_specs=pl.BlockSpec(memory_space=pltpu.VMEM),
        scratch_shapes=[
            pltpu.VMEM((6, 10, 32, 128), BF16),
            pltpu.VMEM((9, 32, 256), BF16),
            pltpu.VMEM((4, 8, 32, 128), BF16),
            pltpu.VMEM((9, 384, 128), BF16),
            pltpu.VMEM((384, 1024), BF16),
            pltpu.VMEM((TAPS, 128, 128), F32),
            pltpu.VMEM((TAPS, 64, 128), F32),
            pltpu.VMEM((TAPS, 64, 128), BF16),
            pltpu.VMEM((3, TAPS, 16, 128), BF16),
            pltpu.VMEM((GROUPS, 4, 16, 128), BF16),
            pltpu.VMEM((NY, 4, 16, 128), BF16),
            pltpu.VMEM((4, 16, 128), F32),
            pltpu.VMEM((NZ, 4, 16, 128), F32),
            dma((4,)), dma((16,)), dma((16,)), dma((10,)), dma((10,)), dma((10, 3)), dma((10, 3)),
            dma((GROUPS,)), dma((NY,)), dma((7,)), dma((7,)), dma((7,)), dma((NY,)),
            dma((GROUPS, 3)), dma((GROUPS, 3)), dma((GROUPS, 4)), dma((GROUPS, 4)),
        ],
        compiler_params=pltpu.CompilerParams(
            collective_id=0, has_side_effects=True, vmem_limit_bytes=40 * 1024 * 1024
        ),
        name="conv_backward",
    )(vol, hid, grad, weights)
    one = out[27, :108].reshape(3, 3, 3, 4, 128).astype(F32)
    grad_one = jnp.transpose(one, (2, 0, 1, 3, 4))
    grad_two = out[:27].reshape(3, 3, 3, 128, 128).astype(F32)
    return (grad_one, grad_two)


def solution(mesh):
    in_specs = (
        P(None, "ha", "wa", None),
        P(None, "ha", "wa", None),
        P(None, "ha", "wa", None),
        P(),
    )
    return jax.shard_map(body, mesh=mesh, in_specs=in_specs, out_specs=(P(), P()), check_vma=False)
```

```python
import jax
import jax.numpy as jnp
from jax import lax
from jax.experimental import pallas as pl
from jax.experimental.pallas import tpu as pltpu
from jax.sharding import PartitionSpec as P

MESH = pl.DeviceIdType.MESH
F32 = jnp.float32
BF16 = jnp.bfloat16
NY, NZ, NX = 8, 8, 4
TAPS = 28
SIDES = [(a, b) for a in (-1, 0, 1) for b in (-1, 0, 1) if (a, b) != (0, 0)]
X_STEPS = (2, 1, 3)
RING = (1, 7, 2, 6, 3, 5, 4)
FAR_FIRST = (6, 5, 4, 3, 2, 1, 0)
LIVE = (8, 6)
SUM = F32
ONE_STEPS = ((1, 2), (0, 2), (1, 1), (1, 3), (0, 1), (0, 3), (1, 0))


def span(side, size):
    if side == 0:
        return slice(0, size), slice(1, size + 1)
    if side == 1:
        return slice(size - 1, size), slice(0, 1)
    return slice(0, 1), slice(size + 1, size + 2)


def kernel(
    vol_ref, hid_ref, go_ref, w_ref, out_ref,
    ext, vols, vol_raw, vol_rows, vol_flat, hid, w, act_t, part, core_rx, x_tx, x_rx,
    one_tx, one_rx, first_tx, first_rx, first_sum, second, stage,
    load_sem, halo_ss, halo_rs, core_ss, core_rs, x_ss, x_rs, o_ss, o_rs, f_ss, f_rs, s_ss, s_rs,
    g_ss, g_rs, xg_ss, xg_rs, cg_ss, cg_rs,
):
    ha = lax.axis_index("ha")
    wa = lax.axis_index("wa")
    ys, core = ha // 2, ha % 2
    zs, xs = wa // 4, wa % 4
    n_ha, n_wa = 2 * NY, NX * NZ

    def dev(y, c, z, x):
        return (y * 2 + c, z * NX + x)

    def near(side):
        return ((ha + side[0] + n_ha) % n_ha, (wa + side[1] + n_wa) % n_wa)

    other = dev(ys, 1 - core, zs, xs)
    x_peer = [dev(ys, core, zs, (xs + i) % NX) for i in X_STEPS]
    cross_peer = [dev(ys, 1 - core, zs, (xs + i) % NX) for i in X_STEPS]
    y_peer = [dev((ys + i) % NY, core, zs, xs) for i in RING]
    z_peer = [dev(ys, core, (zs + i) % NZ, xs) for i in RING]

    loads = [
        pltpu.make_async_copy(vol_ref, vol_raw, load_sem.at[0]),
        pltpu.make_async_copy(hid_ref, hid, load_sem.at[1]),
        pltpu.make_async_copy(go_ref, ext.at[1:5, 1:9], load_sem.at[2]),
        pltpu.make_async_copy(w_ref, w, load_sem.at[3]),
    ]
    for c in loads:
        c.start()

    barrier = pltpu.get_barrier_semaphore()
    greet = [near(s) for s in SIDES] + x_peer + cross_peer + y_peer + z_peer
    for d in greet:
        pl.semaphore_signal(barrier, inc=1, device_id=d, device_id_type=MESH)

    def send(src, dst, ss, rs, device):
        c = pltpu.make_async_remote_copy(
            src_ref=src, dst_ref=dst, send_sem=ss, recv_sem=rs,
            device_id=device, device_id_type=MESH,
        )
        return c

    halo, vol_halo = [], []
    for n, side in enumerate(SIDES):
        (sh, dh), (sw, dw) = span(side[0], 4), span(side[1], 8)
        slot = (1 - side[0]) * 3 + (1 - side[1])
        halo.append(send(go_ref.at[sh, sw], ext.at[dh, dw], halo_ss.at[n], halo_rs.at[n], near(side)))
        vol_halo.append(
            send(vols.at[4], vols.at[slot], halo_ss.at[8 + n], halo_rs.at[8 + n], near(side))
        )

    pl.semaphore_wait(barrier, len(greet))
    for c in halo:
        c.start()

    loads[0].wait()
    vol_rows[...] = jnp.zeros((128, 128), F32)
    vol_rows[:, 0:32] = vol_raw[...].astype(F32).reshape(128, 32)
    halves = []
    for half in range(2):
        lanes = jnp.zeros((16, 128), F32)
        for n in range(4):
            row = vol_rows[pl.ds(half * 4 + n, 16, stride=8), :]
            lanes = lanes + (pltpu.roll(row, 32 * n, 1) if n else row)
        halves.append(lanes)
    vol_flat[...] = jnp.zeros((32, 256), F32)
    for n in range(2):
        for c in range(4):
            for h in range(4):
                vol_flat[h * 8 + c : h * 8 + c + 1, 128 * n : 128 * n + 128] = halves[n][
                    c * 4 + h : c * 4 + h + 1
                ]
    vols[4] = vol_flat[...].astype(BF16)

    for c in vol_halo:
        c.start()

    loads[1].wait()
    depth = lax.broadcasted_iota(jnp.int32, (1024, 128), 0) % 32
    act = jnp.maximum(hid[...], 0).astype(F32).reshape(1024, 128)
    act_t[128:256, :] = act.astype(BF16).T
    lower = jnp.where(depth == 0, 0.0, pltpu.roll(act, 1, 0))
    act_t[0:128, :] = lower.astype(BF16).T
    upper = jnp.where(depth == 31, 0.0, pltpu.roll(act, 1023, 0))
    act_t[256:384, :] = upper.astype(BF16).T
    loads[2].wait()

    def window(g):
        kh, kw = g // 3, g % 3
        return ext[2 - kh : 6 - kh, 2 - kw : 10 - kw].reshape(1024, 128)

    def taps_of(g):
        return slice(3 * g, 3 * g + 3)

    their_half = pl.ds(pl.multiple_of((1 - core) * 64, 64), 64)
    own_half = pl.ds(pl.multiple_of(core * 64, 64), 64)
    own_in_half = pl.ds(pl.multiple_of(xs * 16, 16), 16)
    own_rows = pl.ds(pl.multiple_of(core * 64 + xs * 16, 16), 16)

    core_copies, x_copies = {}, {}

    def core_send(g):
        t = taps_of(g)
        c = send(part.at[t, their_half], core_rx.at[t], core_ss.at[g], core_rs.at[g], other)
        c.start()
        core_copies[g] = c

    def x_send(g):
        t = taps_of(g)
        core_copies[g].wait_recv()
        x_tx[t] = (part[t, own_half] + core_rx[t]).astype(BF16)
        x_copies[g] = []
        for i, step in enumerate(X_STEPS):
            rows = pl.ds(pl.multiple_of((xs + step) % NX * 16, 16), 16)
            c = send(x_tx.at[t, rows], x_rx.at[i, t], x_ss.at[g, i], x_rs.at[g, i], x_peer[i])
            c.start()
            x_copies[g].append(c)

    def grad_two(pair):
        right = jnp.concatenate([window(g) for g in pair], axis=1)
        terms = jnp.dot(act_t[...], right, preferred_element_type=F32)
        for n, g in enumerate(pair):
            part[taps_of(g)] = terms[:, 128 * n : 128 * n + 128].reshape(3, 128, 128)
            core_send(g)

    grad_two((4,))

    for c in halo:
        c.wait_recv()
    for edge, row in ((0, 0), (n_ha - 1, 5)):
        @pl.when(ha == edge)
        def _(row=row):
            ext[row : row + 1] = jnp.zeros((1, 10, 32, 128), BF16)

    for edge, col in ((0, 0), (n_wa - 1, 9)):
        @pl.when(wa == edge)
        def _(col=col):
            ext[:, col : col + 1] = jnp.zeros((6, 1, 32, 128), BF16)

    grad_two((0, 1))
    grad_two((2, 3))
    x_send(4)
    grad_two((5, 6))
    x_send(0)
    x_send(1)
    grad_two((7, 8))
    x_send(2)
    x_send(3)

    for c in vol_halo:
        c.wait_recv()
    for edge, first in ((0, 0), (n_ha - 1, 6)):
        @pl.when(ha == edge)
        def _(first=first):
            vols[first : first + 3] = jnp.zeros((3, 32, 256), BF16)

    for edge, first in ((0, 0), (n_wa - 1, 2)):
        @pl.when(wa == edge)
        def _(first=first):
            for n in (first, first + 3, first + 6):
                vols[n] = jnp.zeros((32, 256), BF16)

    def column(n):
        rows = [vols[n].astype(F32)[24:32], vols[3 + n].astype(F32), vols[6 + n].astype(F32)[0:8]]
        return jnp.concatenate(rows, axis=0)

    left, centre, right = column(0), column(1), column(2)
    lane = lax.broadcasted_iota(jnp.int32, (48, 256), 1)
    by_w = [
        jnp.where(lane < 32, pltpu.roll(left, 32, 1), pltpu.roll(centre, 32, 1)),
        centre,
        jnp.where(lane >= 224, pltpu.roll(right, 224, 1), pltpu.roll(centre, 224, 1)),
    ]
    blocks = []
    for field in by_w:
        blocks.append(jnp.where(lane % 32 == 0, 0.0, pltpu.roll(field, 1, 1)))
        blocks.append(field)
        blocks.append(jnp.where(lane % 32 == 31, 0.0, pltpu.roll(field, 255, 1)))
    fields = jnp.concatenate(blocks, axis=0).astype(BF16)

    loads[3].wait()
    one = [[jnp.zeros((8, 128), F32) for _ in range(3)] for _ in range(9)]
    depth_row = lax.broadcasted_iota(jnp.int32, (256, 128), 0) % 32
    weights = jnp.concatenate([w[g] for g in range(9)], axis=1)
    for h in range(4):
        cells = jnp.concatenate(
            [
                ext[h + 2 - g // 3, 2 - g % 3 : 10 - g % 3].reshape(256, 128)
                for g in range(9)
            ],
            axis=1,
        )
        pulled = lax.dot_general(
            cells, weights, (((1,), (1,)), ((), ())), preferred_element_type=F32
        )
        grad = (
            jnp.where(depth_row == 31, 0.0, pltpu.roll(pulled[:, 0:128], 255, 0))
            + pulled[:, 128:256]
            + jnp.where(depth_row == 0, 0.0, pltpu.roll(pulled[:, 256:384], 1, 0))
        )
        mask = hid[h].reshape(256, 128).astype(F32) > 0
        grad_hidden = jnp.where(mask, grad, 0.0).astype(BF16)
        terms = jnp.dot(fields, grad_hidden, preferred_element_type=F32)
        for b in range(9):
            for kh in range(3):
                first = b * 48 + (h + kh) * 8
                one[b][kh] = one[b][kh] + terms[first : first + 8]
        if h == 0:
            x_send(5)
            x_send(6)
        if h == 1:
            x_send(7)
            x_send(8)
    part[27] = jnp.zeros((128, 128), F32)
    for b in range(9):
        for kh in range(3):
            first = (kh * 9 + b) * 4
            part[27, first : first + 4, :] = one[b][kh][0:4]
    one_tx[...] = part[27].astype(BF16)
    one_copies = []
    for i, (c, step) in enumerate(ONE_STEPS):
        half = core if c == 0 else 1 - core
        rows = pl.ds(pl.multiple_of(half * 64 + (xs + step) % NX * 16, 16), 16)
        device = other if step == 0 else (cross_peer if c else x_peer)[X_STEPS.index(step)]
        one_copies.append(send(one_tx.at[rows], one_rx.at[i], o_ss.at[i], o_rs.at[i], device))
        one_copies[i].start()

    place = (ys, zs)
    peers = (y_peer, z_peer)

    def first_copy(k, j):
        target = dev(j, core, zs, xs) if k == 0 else dev(ys, core, j, xs)
        return send(
            first_tx.at[k, j], first_rx.at[k, place[k]],
            f_ss.at[k, j], f_rs.at[k, place[k]], target,
        )

    seen = set()

    def first_send(k, j):
        lo = 16 * k + 2 * j
        hi = min(lo + 2, 27)
        for g in range(lo // 3, (hi - 1) // 3 + 1):
            if g not in seen:
                seen.add(g)
                for c in x_copies[g]:
                    c.wait_recv()
        t = slice(lo, hi)
        total = part[t, own_rows] + core_rx[t, own_in_half]
        for i in range(3):
            total = total + x_rx[i, t].astype(F32)
        first_sum[t] = total
        if hi == 27:
            one_total = part[27, own_rows]
            for i in range(7):
                one_copies[i].wait_recv()
                one_total = one_total + one_rx[i].astype(F32)
            first_sum[27] = one_total
        first_tx[k, j] = first_sum[lo : lo + 2].astype(BF16)

        @pl.when(place[k] != j)
        def _():
            first_copy(k, j).start()

    def second_copy(k, i):
        at = second.at[k, place[1 - k]]
        return send(at, at, s_ss.at[k, i], s_rs.at[k, i], peers[1 - k][i])

    def second_send(k):
        for s in range(8):
            @pl.when(place[k] != s)
            def _(s=s):
                send(
                    first_tx.at[k, 0], first_rx.at[k, s], f_ss.at[k, 0], f_rs.at[k, s], other
                ).wait_recv()

        total = first_sum[pl.ds(16 * k + 2 * place[k], 2)]
        for s in range(8):
            total = total + jnp.where(place[k] == s, 0.0, first_rx[k, s].astype(F32))
        second[k, place[1 - k]] = total.astype(SUM)
        for i in FAR_FIRST:
            second_copy(k, i).start()

    def gather_copy(k, i):
        return send(
            stage.at[0, k, 0, 0], stage.at[0, k, 0, 1 + i], g_ss.at[k, i], g_rs.at[k, i], peers[k][i]
        )

    def finish(k):
        for i in range(7):
            second_copy(k, i).wait_recv()
        total = second[k, 0].astype(F32)
        for s in range(1, 8):
            total = total + second[k, s].astype(F32)
        stage[0, k, 0, 0] = total.astype(BF16)

    def gather(k):
        for i in FAR_FIRST:
            gather_copy(k, i).start()

    def xg_copy(k, i):
        return send(
            stage.at[0, k, 0], stage.at[0, k, 1 + i], xg_ss.at[k, i], xg_rs.at[k, i], x_peer[i]
        )

    def cg_copy(k, m):
        r = slice(1, 4) if m else slice(0, 1)
        return send(stage.at[0, k, r], stage.at[1, k, r], cg_ss.at[k, m], cg_rs.at[k, m], other)

    def spread(k):
        for i in range(7):
            gather_copy(k, i).wait_recv()
        for i in range(3):
            xg_copy(k, i).start()
        cg_copy(k, 0).start()

    def forward(k):
        for i in range(3):
            xg_copy(k, i).wait_recv()
        cg_copy(k, 1).start()

    def put(c, k, r):
        half = core if c == 0 else 1 - core
        x = xs if r == 0 else (xs + NX - X_STEPS[r - 1]) % NX
        rows = pl.ds(pl.multiple_of(half * 64 + x * 16, 16), 16)
        for s in range(8):
            j = place[k] if s == 0 else (place[k] + 8 - RING[s - 1]) % 8
            out_ref[pl.ds(16 * k + 2 * j, 2), rows] = stage[c, k, r, s]

    live = place[1] < LIVE[1]
    for j in range(LIVE[0]):
        first_send(0, j)
    for j in range(LIVE[1]):
        first_send(1, j)
    second_send(0)
    pl.when(live)(lambda: second_send(1))

    for c in halo + vol_halo:
        c.wait_send()
    for g in range(9):
        core_copies[g].wait_send()

    finish(0)
    gather(0)
    pl.when(live)(lambda: finish(1))

    @pl.when(place[1] >= LIVE[1])
    def _():
        stage[0, 1, 0, 0] = jnp.zeros((2, 16, 128), BF16)

    gather(1)
    for g in range(9):
        for c in x_copies[g]:
            c.wait_send()
    for c in one_copies:
        c.wait_send()
    spread(0)
    spread(1)

    for k in range(2):
        for j in range(LIVE[k]):
            @pl.when(place[k] != j)
            def _(k=k, j=j):
                first_copy(k, j).wait_send()

    def second_left(k):
        for i in range(7):
            second_copy(k, i).wait_send()

    second_left(0)
    pl.when(live)(lambda: second_left(1))
    for k in range(2):
        put(0, k, 0)
        for i in range(7):
            gather_copy(k, i).wait_send()
    forward(0)
    for r in range(1, 4):
        put(0, 0, r)
    cg_copy(0, 0).wait_recv()
    put(1, 0, 0)
    forward(1)
    for r in range(1, 4):
        put(0, 1, r)
    cg_copy(1, 0).wait_recv()
    put(1, 1, 0)
    for k in range(2):
        for i in range(3):
            xg_copy(k, i).wait_send()
        cg_copy(k, 0).wait_send()
    for k in range(2):
        cg_copy(k, 1).wait_recv()
        for r in range(1, 4):
            put(1, k, r)
        cg_copy(k, 1).wait_send()


def widen(sums_ref, one_ref, two_ref, sums, one, two, sem):
    ins = []
    for n in range(4):
        t = slice(7 * n, 7 * n + 7)
        ins.append(pltpu.make_async_copy(sums_ref.at[t], sums.at[t], sem.at[n]))
        ins[n].start()
    outs = []
    for n in range(4):
        ins[n].wait()
        t = slice(7 * n, min(7 * n + 7, 27))
        two[t] = sums[t].astype(F32)
        outs.append(pltpu.make_async_copy(two.at[t], two_ref.at[t], sem.at[4 + n]))
        outs[n].start()
    rows = sums[27].astype(F32)
    for n in range(27):
        one[n] = rows[4 * n : 4 * n + 4]
    outs.append(pltpu.make_async_copy(one, one_ref, sem.at[8]))
    outs[4].start()
    for c in outs:
        c.wait()


def body(volume, hidden_pre, grad_out, weight_two):
    hid = jnp.transpose(hidden_pre, (1, 2, 3, 0))
    grad = jnp.transpose(grad_out, (1, 2, 3, 0))
    weights = weight_two.reshape(9, 384, 128)
    dma = pltpu.SemaphoreType.DMA
    out = pl.pallas_call(
        kernel,
        out_shape=jax.ShapeDtypeStruct((32, 128, 128), BF16),
        in_specs=[pl.BlockSpec(memory_space=pltpu.HBM)] * 4,
        out_specs=pl.BlockSpec(memory_space=pltpu.VMEM),
        scratch_shapes=[
            pltpu.VMEM((6, 10, 32, 128), BF16),
            pltpu.VMEM((9, 32, 256), BF16),
            pltpu.VMEM((4, 4, 8, 32), BF16),
            pltpu.VMEM((128, 128), F32),
            pltpu.VMEM((32, 256), F32),
            pltpu.VMEM((4, 8, 32, 128), BF16),
            pltpu.VMEM((9, 384, 128), BF16),
            pltpu.VMEM((384, 1024), BF16),
            pltpu.VMEM((TAPS, 128, 128), F32),
            pltpu.VMEM((27, 64, 128), F32),
            pltpu.VMEM((27, 64, 128), BF16),
            pltpu.VMEM((3, 27, 16, 128), BF16),
            pltpu.VMEM((128, 128), BF16),
            pltpu.VMEM((7, 16, 128), BF16),
            pltpu.VMEM((2, 8, 2, 16, 128), BF16),
            pltpu.VMEM((2, 8, 2, 16, 128), BF16),
            pltpu.VMEM((TAPS, 16, 128), F32),
            pltpu.VMEM((2, 8, 2, 16, 128), SUM),
            pltpu.VMEM((2, 2, 4, 8, 2, 16, 128), BF16),
            dma((4,)), dma((16,)), dma((16,)), dma((9,)), dma((9,)), dma((9, 3)), dma((9, 3)),
            dma((7,)), dma((7,)), dma((2, 8)), dma((2, 8)), dma((2, 7)), dma((2, 7)), dma((2, 7)), dma((2, 7)),
            dma((2, 3)), dma((2, 3)), dma((2, 2)), dma((2, 2)),
        ],
        compiler_params=pltpu.CompilerParams(
            collective_id=0, has_side_effects=True, vmem_limit_bytes=60 * 1024 * 1024
        ),
        name="conv_backward",
    )(volume, hid, grad, weights)
    one, two = pl.pallas_call(
        widen,
        out_shape=(
            jax.ShapeDtypeStruct((27, 4, 128), F32),
            jax.ShapeDtypeStruct((27, 128, 128), F32),
        ),
        in_specs=[pl.BlockSpec(memory_space=pl.ANY)],
        out_specs=(pl.BlockSpec(memory_space=pl.ANY),) * 2,
        scratch_shapes=[
            pltpu.VMEM((TAPS, 128, 128), BF16),
            pltpu.VMEM((27, 4, 128), F32),
            pltpu.VMEM((27, 128, 128), F32),
            dma((9,)),
        ],
        compiler_params=pltpu.CompilerParams(vmem_limit_bytes=60 * 1024 * 1024),
        name="widen",
    )(out)
    return (one.reshape(3, 3, 3, 4, 128), two.reshape(3, 3, 3, 128, 128))


def solution(mesh):
    in_specs = (
        P(None, "ha", "wa", None),
        P(None, "ha", "wa", None),
        P(None, "ha", "wa", None),
        P(),
    )
    return jax.shard_map(body, mesh=mesh, in_specs=in_specs, out_specs=(P(), P()), check_vma=False)
```

```python
import jax
import jax.numpy as jnp
from jax import lax
from jax.experimental import pallas as pl
from jax.experimental.pallas import tpu as pltpu
from jax.sharding import PartitionSpec as P

MESH = pl.DeviceIdType.MESH
F32 = jnp.float32
BF16 = jnp.bfloat16
NY, NZ, NX = 8, 8, 4
TAPS = 28
SIDES = [(a, b) for a in (-1, 0, 1) for b in (-1, 0, 1) if (a, b) != (0, 0)]
X_STEPS = (2, 1, 3)
RING = (1, 7, 2, 6, 3, 5, 4)
FAR_FIRST = (6, 5, 4, 3, 2, 1, 0)
LIVE = (8, 6)
SUM = F32
ONE_STEPS = ((1, 2), (0, 2), (1, 1), (1, 3), (0, 1), (0, 3), (1, 0))


def span(side, size):
    if side == 0:
        return slice(0, size), slice(1, size + 1)
    if side == 1:
        return slice(size - 1, size), slice(0, 1)
    return slice(0, 1), slice(size + 1, size + 2)


def kernel(
    vol_ref, hid_ref, go_ref, w_ref, out_ref,
    ext, vols, vol_raw, vol_rows, vol_flat, hid, w, act_t, part, core_rx, x_tx, x_rx,
    one_tx, one_rx, first_tx, first_rx, first_sum, second, stage,
    load_sem, halo_ss, halo_rs, core_ss, core_rs, x_ss, x_rs, o_ss, o_rs, f_ss, f_rs, s_ss, s_rs,
    g_ss, g_rs, xg_ss, xg_rs, cg_ss, cg_rs,
):
    ha = lax.axis_index("ha")
    wa = lax.axis_index("wa")
    ys, core = ha // 2, ha % 2
    zs, xs = wa // 4, wa % 4
    n_ha, n_wa = 2 * NY, NX * NZ

    def dev(y, c, z, x):
        return (y * 2 + c, z * NX + x)

    def near(side):
        return ((ha + side[0] + n_ha) % n_ha, (wa + side[1] + n_wa) % n_wa)

    other = dev(ys, 1 - core, zs, xs)
    x_peer = [dev(ys, core, zs, (xs + i) % NX) for i in X_STEPS]
    cross_peer = [dev(ys, 1 - core, zs, (xs + i) % NX) for i in X_STEPS]
    y_peer = [dev((ys + i) % NY, core, zs, xs) for i in RING]
    z_peer = [dev(ys, core, (zs + i) % NZ, xs) for i in RING]

    loads = [
        pltpu.make_async_copy(vol_ref, vol_raw, load_sem.at[0]),
        pltpu.make_async_copy(hid_ref, hid, load_sem.at[1]),
        pltpu.make_async_copy(go_ref, ext.at[1:5, 1:9], load_sem.at[2]),
        pltpu.make_async_copy(w_ref, w, load_sem.at[3]),
    ]
    for c in loads:
        c.start()

    barrier = pltpu.get_barrier_semaphore()
    greet = [near(s) for s in SIDES] + x_peer + cross_peer + y_peer + z_peer
    for d in greet:
        pl.semaphore_signal(barrier, inc=1, device_id=d, device_id_type=MESH)

    def send(src, dst, ss, rs, device):
        c = pltpu.make_async_remote_copy(
            src_ref=src, dst_ref=dst, send_sem=ss, recv_sem=rs,
            device_id=device, device_id_type=MESH,
        )
        return c

    halo, vol_halo = [], []
    for n, side in enumerate(SIDES):
        (sh, dh), (sw, dw) = span(side[0], 4), span(side[1], 8)
        slot = (1 - side[0]) * 3 + (1 - side[1])
        halo.append(send(go_ref.at[sh, sw], ext.at[dh, dw], halo_ss.at[n], halo_rs.at[n], near(side)))
        vol_halo.append(
            send(vols.at[4], vols.at[slot], halo_ss.at[8 + n], halo_rs.at[8 + n], near(side))
        )

    pl.semaphore_wait(barrier, len(greet))
    for c in halo:
        c.start()

    loads[0].wait()
    vol_rows[...] = jnp.zeros((128, 128), F32)
    vol_rows[:, 0:32] = vol_raw[...].astype(F32).reshape(128, 32)
    halves = []
    for half in range(2):
        lanes = jnp.zeros((16, 128), F32)
        for n in range(4):
            row = vol_rows[pl.ds(half * 4 + n, 16, stride=8), :]
            lanes = lanes + (pltpu.roll(row, 32 * n, 1) if n else row)
        halves.append(lanes)
    vol_flat[...] = jnp.zeros((32, 256), F32)
    for n in range(2):
        for c in range(4):
            for h in range(4):
                vol_flat[h * 8 + c : h * 8 + c + 1, 128 * n : 128 * n + 128] = halves[n][
                    c * 4 + h : c * 4 + h + 1
                ]
    vols[4] = vol_flat[...].astype(BF16)

    for c in vol_halo:
        c.start()

    loads[1].wait()
    depth = lax.broadcasted_iota(jnp.int32, (1024, 128), 0) % 32
    act = jnp.maximum(hid[...], 0).astype(F32).reshape(1024, 128)
    act_t[128:256, :] = act.astype(BF16).T
    lower = jnp.where(depth == 0, 0.0, pltpu.roll(act, 1, 0))
    act_t[0:128, :] = lower.astype(BF16).T
    upper = jnp.where(depth == 31, 0.0, pltpu.roll(act, 1023, 0))
    act_t[256:384, :] = upper.astype(BF16).T
    loads[2].wait()

    def window(g):
        kh, kw = g // 3, g % 3
        return ext[2 - kh : 6 - kh, 2 - kw : 10 - kw].reshape(1024, 128)

    def taps_of(g):
        return slice(3 * g, 3 * g + 3)

    their_half = pl.ds(pl.multiple_of((1 - core) * 64, 64), 64)
    own_half = pl.ds(pl.multiple_of(core * 64, 64), 64)
    own_in_half = pl.ds(pl.multiple_of(xs * 16, 16), 16)
    own_rows = pl.ds(pl.multiple_of(core * 64 + xs * 16, 16), 16)

    core_copies, x_copies = {}, {}

    def core_send(g):
        t = taps_of(g)
        c = send(part.at[t, their_half], core_rx.at[t], core_ss.at[g], core_rs.at[g], other)
        c.start()
        core_copies[g] = c

    def x_send(g):
        t = taps_of(g)
        core_copies[g].wait_recv()
        x_tx[t] = (part[t, own_half] + core_rx[t]).astype(BF16)
        x_copies[g] = []
        for i, step in enumerate(X_STEPS):
            rows = pl.ds(pl.multiple_of((xs + step) % NX * 16, 16), 16)
            c = send(x_tx.at[t, rows], x_rx.at[i, t], x_ss.at[g, i], x_rs.at[g, i], x_peer[i])
            c.start()
            x_copies[g].append(c)

    def grad_two(pair):
        right = jnp.concatenate([window(g) for g in pair], axis=1)
        terms = jnp.dot(act_t[...], right, preferred_element_type=F32)
        for n, g in enumerate(pair):
            part[taps_of(g)] = terms[:, 128 * n : 128 * n + 128].reshape(3, 128, 128)
            core_send(g)

    grad_two((4,))

    for c in halo:
        c.wait_recv()
    for edge, row in ((0, 0), (n_ha - 1, 5)):
        @pl.when(ha == edge)
        def _(row=row):
            ext[row : row + 1] = jnp.zeros((1, 10, 32, 128), BF16)

    for edge, col in ((0, 0), (n_wa - 1, 9)):
        @pl.when(wa == edge)
        def _(col=col):
            ext[:, col : col + 1] = jnp.zeros((6, 1, 32, 128), BF16)

    grad_two((0, 1))
    grad_two((2, 3))
    x_send(4)
    grad_two((5, 6))
    x_send(0)
    x_send(1)
    grad_two((7, 8))
    x_send(2)
    x_send(3)

    for c in vol_halo:
        c.wait_recv()
    for edge, first in ((0, 0), (n_ha - 1, 6)):
        @pl.when(ha == edge)
        def _(first=first):
            vols[first : first + 3] = jnp.zeros((3, 32, 256), BF16)

    for edge, first in ((0, 0), (n_wa - 1, 2)):
        @pl.when(wa == edge)
        def _(first=first):
            for n in (first, first + 3, first + 6):
                vols[n] = jnp.zeros((32, 256), BF16)

    def column(n):
        rows = [vols[n].astype(F32)[24:32], vols[3 + n].astype(F32), vols[6 + n].astype(F32)[0:8]]
        return jnp.concatenate(rows, axis=0)

    left, centre, right = column(0), column(1), column(2)
    lane = lax.broadcasted_iota(jnp.int32, (48, 256), 1)
    by_w = [
        jnp.where(lane < 32, pltpu.roll(left, 32, 1), pltpu.roll(centre, 32, 1)),
        centre,
        jnp.where(lane >= 224, pltpu.roll(right, 224, 1), pltpu.roll(centre, 224, 1)),
    ]
    blocks = []
    for field in by_w:
        blocks.append(jnp.where(lane % 32 == 0, 0.0, pltpu.roll(field, 1, 1)))
        blocks.append(field)
        blocks.append(jnp.where(lane % 32 == 31, 0.0, pltpu.roll(field, 255, 1)))

    loads[3].wait()
    one = [[jnp.zeros((8, 128), F32) for _ in range(3)] for _ in range(9)]
    depth_row = lax.broadcasted_iota(jnp.int32, (256, 128), 0) % 32
    weights = jnp.concatenate([w[g] for g in range(9)], axis=1)
    for h in range(4):
        cells = jnp.concatenate(
            [
                ext[h + 2 - g // 3, 2 - g % 3 : 10 - g % 3].reshape(256, 128)
                for g in range(9)
            ],
            axis=1,
        )
        pulled = lax.dot_general(
            cells, weights, (((1,), (1,)), ((), ())), preferred_element_type=F32
        )
        grad = (
            jnp.where(depth_row == 31, 0.0, pltpu.roll(pulled[:, 0:128], 255, 0))
            + pulled[:, 128:256]
            + jnp.where(depth_row == 0, 0.0, pltpu.roll(pulled[:, 256:384], 1, 0))
        )
        mask = hid[h].reshape(256, 128).astype(F32) > 0
        grad_hidden = jnp.where(mask, grad, 0.0).astype(BF16)
        fields = jnp.concatenate([block[8 * h : 8 * h + 24] for block in blocks], axis=0)
        terms = jnp.dot(fields.astype(BF16), grad_hidden, preferred_element_type=F32)
        for b in range(9):
            for kh in range(3):
                first = b * 24 + kh * 8
                one[b][kh] = one[b][kh] + terms[first : first + 8]
        if h == 0:
            x_send(5)
            x_send(6)
        if h == 1:
            x_send(7)
            x_send(8)
    part[27] = jnp.zeros((128, 128), F32)
    for b in range(9):
        for kh in range(3):
            first = (kh * 9 + b) * 4
            part[27, first : first + 4, :] = one[b][kh][0:4]
    one_tx[...] = part[27].astype(BF16)
    one_copies = []
    for i, (c, step) in enumerate(ONE_STEPS):
        half = core if c == 0 else 1 - core
        rows = pl.ds(pl.multiple_of(half * 64 + (xs + step) % NX * 16, 16), 16)
        device = other if step == 0 else (cross_peer if c else x_peer)[X_STEPS.index(step)]
        one_copies.append(send(one_tx.at[rows], one_rx.at[i], o_ss.at[i], o_rs.at[i], device))
        one_copies[i].start()

    place = (ys, zs)
    peers = (y_peer, z_peer)

    def first_copy(k, o, n):
        j = (place[k] + o) % 8
        target = dev(j, core, zs, xs) if k == 0 else dev(ys, core, j, xs)
        return send(first_tx.at[k, j], first_rx.at[k, o], f_ss.at[k, n], f_rs.at[k, o], target)

    seen = set()

    def first_total(k, j):
        lo = 16 * k + 2 * j
        hi = min(lo + 2, 27)
        for g in range(lo // 3, (hi - 1) // 3 + 1):
            if g not in seen:
                seen.add(g)
                for c in x_copies[g]:
                    c.wait_recv()
        t = slice(lo, hi)
        total = part[t, own_rows] + core_rx[t, own_in_half]
        for i in range(3):
            total = total + x_rx[i, t].astype(F32)
        first_sum[t] = total
        if hi == 27:
            one_total = part[27, own_rows]
            for i in range(7):
                one_copies[i].wait_recv()
                one_total = one_total + one_rx[i].astype(F32)
            first_sum[27] = one_total
        first_tx[k, j] = first_sum[lo : lo + 2].astype(BF16)

    last = LIVE[1] - 1
    last_step = (last + 8 - zs) % 8

    def early(n):
        return (zs + RING[n]) % 8 < last

    def second_copy(k, i):
        at = second.at[k, place[1 - k]]
        return send(at, at, s_ss.at[k, i], s_rs.at[k, i], peers[1 - k][i])

    def second_send(k):
        for n in range(7):
            first_copy(k, RING[n], n).wait_recv()
        total = first_sum[pl.ds(16 * k + 2 * place[k], 2)]
        for n in range(7):
            total = total + first_rx[k, RING[n]].astype(F32)
        second[k, place[1 - k]] = total.astype(SUM)
        for i in FAR_FIRST:
            second_copy(k, i).start()

    def gather_copy(k, i):
        return send(
            stage.at[0, k, 0, 0], stage.at[0, k, 0, 1 + i], g_ss.at[k, i], g_rs.at[k, i], peers[k][i]
        )

    def finish(k):
        for i in range(7):
            second_copy(k, i).wait_recv()
        total = second[k, 0].astype(F32)
        for s in range(1, 8):
            total = total + second[k, s].astype(F32)
        stage[0, k, 0, 0] = total.astype(BF16)

    def gather(k):
        for i in FAR_FIRST:
            gather_copy(k, i).start()

    def xg_copy(k, i):
        return send(
            stage.at[0, k, 0], stage.at[0, k, 1 + i], xg_ss.at[k, i], xg_rs.at[k, i], x_peer[i]
        )

    def cg_copy(k, m):
        r = slice(1, 4) if m else slice(0, 1)
        return send(stage.at[0, k, r], stage.at[1, k, r], cg_ss.at[k, m], cg_rs.at[k, m], other)

    def spread(k):
        for i in range(7):
            gather_copy(k, i).wait_recv()
        for i in range(3):
            xg_copy(k, i).start()
        cg_copy(k, 0).start()

    def forward(k):
        for i in range(3):
            xg_copy(k, i).wait_recv()
        cg_copy(k, 1).start()

    def put(c, k, r):
        half = core if c == 0 else 1 - core
        x = xs if r == 0 else (xs + NX - X_STEPS[r - 1]) % NX
        rows = pl.ds(pl.multiple_of(half * 64 + x * 16, 16), 16)
        for s in range(8):
            j = place[k] if s == 0 else (place[k] + 8 - RING[s - 1]) % 8
            out_ref[pl.ds(16 * k + 2 * j, 2), rows] = stage[c, k, r, s]

    live = place[1] < LIVE[1]
    for j in range(LIVE[0]):
        first_total(0, j)
    for n in FAR_FIRST:
        first_copy(0, RING[n], n).start()
    for j in range(last):
        first_total(1, j)
    for n in FAR_FIRST:
        pl.when(early(n))(lambda n=n: first_copy(1, RING[n], n).start())
    first_total(1, last)
    pl.when(zs != last)(lambda: first_copy(1, last_step, 7).start())
    second_send(0)
    pl.when(live)(lambda: second_send(1))

    for c in halo + vol_halo:
        c.wait_send()
    for g in range(9):
        core_copies[g].wait_send()

    finish(0)
    gather(0)
    pl.when(live)(lambda: finish(1))

    @pl.when(place[1] >= LIVE[1])
    def _():
        stage[0, 1, 0, 0] = jnp.zeros((2, 16, 128), BF16)

    gather(1)
    for g in range(9):
        for c in x_copies[g]:
            c.wait_send()
    for c in one_copies:
        c.wait_send()
    spread(0)
    spread(1)

    for n in range(7):
        first_copy(0, RING[n], n).wait_send()
    for n in range(7):
        pl.when(early(n))(lambda n=n: first_copy(1, RING[n], n).wait_send())
    pl.when(zs != last)(lambda: first_copy(1, last_step, 7).wait_send())

    def second_left(k):
        for i in range(7):
            second_copy(k, i).wait_send()

    second_left(0)
    pl.when(live)(lambda: second_left(1))
    for k in range(2):
        put(0, k, 0)
        for i in range(7):
            gather_copy(k, i).wait_send()
    forward(0)
    for r in range(1, 4):
        put(0, 0, r)
    cg_copy(0, 0).wait_recv()
    put(1, 0, 0)
    forward(1)
    for r in range(1, 4):
        put(0, 1, r)
    cg_copy(1, 0).wait_recv()
    put(1, 1, 0)
    for k in range(2):
        for i in range(3):
            xg_copy(k, i).wait_send()
        cg_copy(k, 0).wait_send()
    for k in range(2):
        cg_copy(k, 1).wait_recv()
        for r in range(1, 4):
            put(1, k, r)
        cg_copy(k, 1).wait_send()


def widen(sums_ref, one_ref, two_ref, one, two, sem):
    outs = []
    for n in range(4):
        t = slice(7 * n, min(7 * n + 7, 27))
        two[t] = sums_ref[t].astype(F32)
        outs.append(pltpu.make_async_copy(two.at[t], two_ref.at[t], sem.at[n]))
        outs[n].start()
    rows = sums_ref[27].astype(F32)
    for n in range(27):
        one[n] = rows[4 * n : 4 * n + 4]
    outs.append(pltpu.make_async_copy(one, one_ref, sem.at[4]))
    outs[4].start()
    for c in outs:
        c.wait()


def body(volume, hidden_pre, grad_out, weight_two):
    hid = jnp.transpose(hidden_pre, (1, 2, 3, 0))
    grad = jnp.transpose(grad_out, (1, 2, 3, 0))
    weights = weight_two.reshape(9, 384, 128)
    dma = pltpu.SemaphoreType.DMA
    out = pl.pallas_call(
        kernel,
        out_shape=jax.ShapeDtypeStruct((32, 128, 128), BF16),
        in_specs=[pl.BlockSpec(memory_space=pltpu.HBM)] * 4,
        out_specs=pl.BlockSpec(memory_space=pltpu.VMEM),
        scratch_shapes=[
            pltpu.VMEM((6, 10, 32, 128), BF16),
            pltpu.VMEM((9, 32, 256), BF16),
            pltpu.VMEM((4, 4, 8, 32), BF16),
            pltpu.VMEM((128, 128), F32),
            pltpu.VMEM((32, 256), F32),
            pltpu.VMEM((4, 8, 32, 128), BF16),
            pltpu.VMEM((9, 384, 128), BF16),
            pltpu.VMEM((384, 1024), BF16),
            pltpu.VMEM((TAPS, 128, 128), F32),
            pltpu.VMEM((27, 64, 128), F32),
            pltpu.VMEM((27, 64, 128), BF16),
            pltpu.VMEM((3, 27, 16, 128), BF16),
            pltpu.VMEM((128, 128), BF16),
            pltpu.VMEM((7, 16, 128), BF16),
            pltpu.VMEM((2, 8, 2, 16, 128), BF16),
            pltpu.VMEM((2, 8, 2, 16, 128), BF16),
            pltpu.VMEM((TAPS, 16, 128), F32),
            pltpu.VMEM((2, 8, 2, 16, 128), SUM),
            pltpu.VMEM((2, 2, 4, 8, 2, 16, 128), BF16),
            dma((4,)), dma((16,)), dma((16,)), dma((9,)), dma((9,)), dma((9, 3)), dma((9, 3)),
            dma((7,)), dma((7,)), dma((2, 8)), dma((2, 8)), dma((2, 7)), dma((2, 7)), dma((2, 7)), dma((2, 7)),
            dma((2, 3)), dma((2, 3)), dma((2, 2)), dma((2, 2)),
        ],
        compiler_params=pltpu.CompilerParams(
            collective_id=0, has_side_effects=True, vmem_limit_bytes=44 * 1024 * 1024
        ),
        name="conv_backward",
    )(*[pltpu.with_memory_space_constraint(x, pltpu.HBM) for x in (volume, hid, grad, weights)])
    one, two = pl.pallas_call(
        widen,
        out_shape=(
            jax.ShapeDtypeStruct((27, 4, 128), F32),
            jax.ShapeDtypeStruct((27, 128, 128), F32),
        ),
        in_specs=[pl.BlockSpec(memory_space=pltpu.VMEM)],
        out_specs=(pl.BlockSpec(memory_space=pl.ANY),) * 2,
        scratch_shapes=[
            pltpu.VMEM((27, 4, 128), F32),
            pltpu.VMEM((27, 128, 128), F32),
            dma((5,)),
        ],
        compiler_params=pltpu.CompilerParams(vmem_limit_bytes=8 * 1024 * 1024),
        name="widen",
    )(out)
    return (one.reshape(3, 3, 3, 4, 128), two.reshape(3, 3, 3, 128, 128))


def solution(mesh):
    in_specs = (
        P(None, "ha", "wa", None),
        P(None, "ha", "wa", None),
        P(None, "ha", "wa", None),
        P(),
    )
    return jax.shard_map(body, mesh=mesh, in_specs=in_specs, out_specs=(P(), P()), check_vma=False)
```

```python
import jax
import jax.numpy as jnp
from jax import lax
from jax.experimental import pallas as pl
from jax.experimental.pallas import tpu as pltpu
from jax.sharding import PartitionSpec as P

MESH = pl.DeviceIdType.MESH
F32 = jnp.float32
BF16 = jnp.bfloat16
NY, NZ, NX = 8, 8, 4
TAPS = 28
SIDES = [(a, b) for a in (-1, 0, 1) for b in (-1, 0, 1) if (a, b) != (0, 0)]
X_STEPS = (2, 1, 3)
RING = (1, 7, 2, 6, 3, 5, 4)
FAR_FIRST = (6, 5, 4, 3, 2, 1, 0)
LIVE = (8, 6)
SUM = BF16
PARTS = ((0, 0, 8), (1, 0, 5), (1, 5, 6))
ONE_STEPS = ((1, 2), (0, 2), (1, 1), (1, 3), (0, 1), (0, 3), (1, 0))


def span(side, size):
    if side == 0:
        return slice(0, size), slice(1, size + 1)
    if side == 1:
        return slice(size - 1, size), slice(0, 1)
    return slice(0, 1), slice(size + 1, size + 2)


def kernel(
    vol_ref, hid_ref, go_ref, w_ref, out_ref,
    ext, vols, vol_raw, vol_rows, vol_flat, hid, w, act_t, part, core_rx, x_tx, x_rx,
    one_rx, first_tx, first_rx, first_sum, second, stage,
    load_sem, halo_ss, halo_rs, core_ss, core_rs, x_ss, x_rs, o_ss, o_rs, f_ss, f_rs, s_ss, s_rs,
    g_ss, g_rs, xg_ss, xg_rs, cg_ss, cg_rs,
):
    ha = lax.axis_index("ha")
    wa = lax.axis_index("wa")
    ys, core = ha // 2, ha % 2
    zs, xs = wa // 4, wa % 4
    n_ha, n_wa = 2 * NY, NX * NZ

    def dev(y, c, z, x):
        return (y * 2 + c, z * NX + x)

    def near(side):
        return ((ha + side[0] + n_ha) % n_ha, (wa + side[1] + n_wa) % n_wa)

    other = dev(ys, 1 - core, zs, xs)
    x_peer = [dev(ys, core, zs, (xs + i) % NX) for i in X_STEPS]
    cross_peer = [dev(ys, 1 - core, zs, (xs + i) % NX) for i in X_STEPS]
    y_peer = [dev((ys + i) % NY, core, zs, xs) for i in RING]
    z_peer = [dev(ys, core, (zs + i) % NZ, xs) for i in RING]

    barrier = pltpu.get_barrier_semaphore()
    greet = [p[i] for i in FAR_FIRST for p in (z_peer, y_peer)]
    greet += cross_peer + x_peer + [near(s) for s in SIDES]
    for d in greet:
        pl.semaphore_signal(barrier, inc=1, device_id=d, device_id_type=MESH)

    loads = [
        pltpu.make_async_copy(vol_ref, vol_raw, load_sem.at[0]),
        pltpu.make_async_copy(hid_ref, hid, load_sem.at[1]),
        pltpu.make_async_copy(go_ref, ext.at[1:5, 1:9], load_sem.at[2]),
        pltpu.make_async_copy(w_ref, w, load_sem.at[3]),
    ]
    for c in loads:
        c.start()

    def send(src, dst, ss, rs, device):
        c = pltpu.make_async_remote_copy(
            src_ref=src, dst_ref=dst, send_sem=ss, recv_sem=rs,
            device_id=device, device_id_type=MESH,
        )
        return c

    halo, vol_halo = [], []
    for n, side in enumerate(SIDES):
        (sh, dh), (sw, dw) = span(side[0], 4), span(side[1], 8)
        slot = (1 - side[0]) * 3 + (1 - side[1])
        halo.append(send(go_ref.at[sh, sw], ext.at[dh, dw], halo_ss.at[n], halo_rs.at[n], near(side)))
        vol_halo.append(
            send(vols.at[4], vols.at[slot], halo_ss.at[8 + n], halo_rs.at[8 + n], near(side))
        )

    pl.semaphore_wait(barrier, len(greet))
    for c in halo:
        c.start()

    loads[0].wait()
    vol_rows[...] = jnp.zeros((128, 128), F32)
    vol_rows[:, 0:32] = vol_raw[...].astype(F32).reshape(128, 32)
    halves = []
    for half in range(2):
        lanes = jnp.zeros((16, 128), F32)
        for n in range(4):
            row = vol_rows[pl.ds(half * 4 + n, 16, stride=8), :]
            lanes = lanes + (pltpu.roll(row, 32 * n, 1) if n else row)
        halves.append(lanes)
    vol_flat[...] = jnp.zeros((32, 256), F32)
    for n in range(2):
        for c in range(4):
            for h in range(4):
                vol_flat[h * 8 + c : h * 8 + c + 1, 128 * n : 128 * n + 128] = halves[n][
                    c * 4 + h : c * 4 + h + 1
                ]
    vols[4] = vol_flat[...].astype(BF16)

    for c in vol_halo:
        c.start()

    loads[1].wait()
    depth = lax.broadcasted_iota(jnp.int32, (1024, 128), 0) % 32
    act = jnp.maximum(hid[...], 0).astype(F32).reshape(1024, 128)
    act_t[128:256, :] = act.astype(BF16).T
    lower = jnp.where(depth == 0, 0.0, pltpu.roll(act, 1, 0))
    act_t[0:128, :] = lower.astype(BF16).T
    upper = jnp.where(depth == 31, 0.0, pltpu.roll(act, 1023, 0))
    act_t[256:384, :] = upper.astype(BF16).T
    loads[2].wait()

    def window(g):
        kh, kw = g // 3, g % 3
        return ext[2 - kh : 6 - kh, 2 - kw : 10 - kw].reshape(1024, 128)

    def taps_of(g):
        return slice(3 * g, 3 * g + 3)

    their_half = pl.ds(pl.multiple_of((1 - core) * 64, 64), 64)
    own_half = pl.ds(pl.multiple_of(core * 64, 64), 64)
    own_in_half = pl.ds(pl.multiple_of(xs * 16, 16), 16)
    own_rows = pl.ds(pl.multiple_of(core * 64 + xs * 16, 16), 16)

    core_copies, x_copies = {}, {}

    def core_send(g):
        t = taps_of(g)
        c = send(part.at[t, their_half], core_rx.at[t], core_ss.at[g], core_rs.at[g], other)
        c.start()
        core_copies[g] = c

    def x_send(g):
        t = taps_of(g)
        core_copies[g].wait_recv()
        x_tx[t] = (part[t, own_half] + core_rx[t]).astype(BF16)
        x_copies[g] = []
        for i, step in enumerate(X_STEPS):
            rows = pl.ds(pl.multiple_of((xs + step) % NX * 16, 16), 16)
            c = send(x_tx.at[t, rows], x_rx.at[i, t], x_ss.at[g, i], x_rs.at[g, i], x_peer[i])
            c.start()
            x_copies[g].append(c)

    def grad_two(pair):
        right = jnp.concatenate([window(g) for g in pair], axis=1)
        terms = jnp.dot(act_t[...], right, preferred_element_type=F32)
        for n, g in enumerate(pair):
            part[taps_of(g)] = terms[:, 128 * n : 128 * n + 128].reshape(3, 128, 128)
            core_send(g)

    grad_two((4,))

    for c in halo:
        c.wait_recv()
    for edge, row in ((0, 0), (n_ha - 1, 5)):
        @pl.when(ha == edge)
        def _(row=row):
            ext[row : row + 1] = jnp.zeros((1, 10, 32, 128), BF16)

    for edge, col in ((0, 0), (n_wa - 1, 9)):
        @pl.when(wa == edge)
        def _(col=col):
            ext[:, col : col + 1] = jnp.zeros((6, 1, 32, 128), BF16)

    grad_two((0, 1))
    grad_two((2, 3))
    x_send(4)
    grad_two((5, 6))
    x_send(0)
    x_send(1)
    grad_two((7, 8))
    x_send(2)
    x_send(3)

    for c in vol_halo:
        c.wait_recv()
    for edge, first in ((0, 0), (n_ha - 1, 6)):
        @pl.when(ha == edge)
        def _(first=first):
            vols[first : first + 3] = jnp.zeros((3, 32, 256), BF16)

    for edge, first in ((0, 0), (n_wa - 1, 2)):
        @pl.when(wa == edge)
        def _(first=first):
            for n in (first, first + 3, first + 6):
                vols[n] = jnp.zeros((32, 256), BF16)

    def column(n):
        rows = [vols[n].astype(F32)[24:32], vols[3 + n].astype(F32), vols[6 + n].astype(F32)[0:8]]
        return jnp.concatenate(rows, axis=0)

    left, centre, right = column(0), column(1), column(2)
    lane = lax.broadcasted_iota(jnp.int32, (48, 256), 1)
    by_w = [
        jnp.where(lane < 32, pltpu.roll(left, 32, 1), pltpu.roll(centre, 32, 1)),
        centre,
        jnp.where(lane >= 224, pltpu.roll(right, 224, 1), pltpu.roll(centre, 224, 1)),
    ]
    blocks = []
    for field in by_w:
        blocks.append(jnp.where(lane % 32 == 0, 0.0, pltpu.roll(field, 1, 1)))
        blocks.append(field)
        blocks.append(jnp.where(lane % 32 == 31, 0.0, pltpu.roll(field, 255, 1)))

    loads[3].wait()
    one = [[jnp.zeros((8, 128), F32) for _ in range(3)] for _ in range(9)]
    depth_row = lax.broadcasted_iota(jnp.int32, (256, 128), 0) % 32
    weights = jnp.concatenate([w[g] for g in range(9)], axis=1)
    for h in range(4):
        cells = jnp.concatenate(
            [
                ext[h + 2 - g // 3, 2 - g % 3 : 10 - g % 3].reshape(256, 128)
                for g in range(9)
            ],
            axis=1,
        )
        pulled = lax.dot_general(
            cells, weights, (((1,), (1,)), ((), ())), preferred_element_type=F32
        )
        grad = (
            jnp.where(depth_row == 31, 0.0, pltpu.roll(pulled[:, 0:128], 255, 0))
            + pulled[:, 128:256]
            + jnp.where(depth_row == 0, 0.0, pltpu.roll(pulled[:, 256:384], 1, 0))
        )
        mask = hid[h].reshape(256, 128).astype(F32) > 0
        grad_hidden = jnp.where(mask, grad, 0.0).astype(BF16)
        fields = jnp.concatenate([block[8 * h : 8 * h + 24] for block in blocks], axis=0)
        terms = jnp.dot(fields.astype(BF16), grad_hidden, preferred_element_type=F32)
        for b in range(9):
            for kh in range(3):
                first = b * 24 + kh * 8
                one[b][kh] = one[b][kh] + terms[first : first + 8]
        if h == 0:
            x_send(5)
            x_send(6)
        if h == 1:
            x_send(7)
            x_send(8)
    part[27] = jnp.zeros((128, 128), F32)
    for b in range(9):
        for kh in range(3):
            first = (kh * 9 + b) * 4
            part[27, first : first + 4, :] = one[b][kh][0:4]
    one_copies = []
    for i, (c, step) in enumerate(ONE_STEPS):
        half = core if c == 0 else 1 - core
        rows = pl.ds(pl.multiple_of(half * 64 + (xs + step) % NX * 16, 16), 16)
        device = other if step == 0 else (cross_peer if c else x_peer)[X_STEPS.index(step)]
        one_copies.append(send(part.at[27, rows], one_rx.at[i], o_ss.at[i], o_rs.at[i], device))
        one_copies[i].start()

    place = (ys, zs)
    peers = (y_peer, z_peer)

    def first_copy(k, o, n):
        j = (place[k] + o) % 8
        target = dev(j, core, zs, xs) if k == 0 else dev(ys, core, j, xs)
        return send(first_tx.at[k, j], first_rx.at[k, o], f_ss.at[k, n], f_rs.at[k, o], target)

    seen = set()

    def first_total(k, j):
        lo = 16 * k + 2 * j
        hi = min(lo + 2, 27)
        for g in range(lo // 3, (hi - 1) // 3 + 1):
            if g not in seen:
                seen.add(g)
                for c in x_copies[g]:
                    c.wait_recv()
        t = slice(lo, hi)
        total = part[t, own_rows] + core_rx[t, own_in_half]
        for i in range(3):
            total = total + x_rx[i, t].astype(F32)
        first_sum[t] = total
        if hi == 27:
            one_total = part[27, own_rows]
            for i in range(7):
                one_copies[i].wait_recv()
                one_total = one_total + one_rx[i]
            first_sum[27] = one_total
        first_tx[k, j] = first_sum[lo : lo + 2].astype(BF16)

    last = LIVE[1] - 1
    last_step = (last + 8 - zs) % 8

    def early(n):
        return (zs + RING[n]) % 8 < last

    def second_copy(k, i):
        at = second.at[k, place[1 - k]]
        return send(at, at, s_ss.at[k, i], s_rs.at[k, i], peers[1 - k][i])

    def second_send(k):
        for n in range(7):
            first_copy(k, RING[n], n).wait_recv()
        total = first_sum[pl.ds(16 * k + 2 * place[k], 2)]
        for n in range(7):
            total = total + first_rx[k, RING[n]].astype(F32)
        second[k, place[1 - k]] = total.astype(SUM)
        for i in FAR_FIRST:
            second_copy(k, i).start()

    def gather_copy(k, i):
        if k == 0:
            return send(
                stage.at[0, 0, 0, 0], stage.at[0, 0, 0, 1 + i],
                g_ss.at[0, i], g_rs.at[0, i], y_peer[i],
            )
        at = stage.at[0, 1, 0, zs]
        return send(at, at, g_ss.at[1, i], g_rs.at[1, zs], z_peer[i])

    def gathered(j):
        at = stage.at[0, 1, 0, j]
        pl.when(zs != j)(lambda: send(at, at, g_ss.at[1, 0], g_rs.at[1, j], other).wait_recv())

    def finish(k):
        for i in range(7):
            second_copy(k, i).wait_recv()
        total = second[k, 0].astype(F32)
        for s in range(1, 8):
            total = total + second[k, s].astype(F32)
        stage[0, k, 0, k * zs] = total.astype(BF16)

    def gather(k):
        for i in FAR_FIRST:
            gather_copy(k, i).start()

    def xg_copy(p, i):
        k, lo, hi = PARTS[p]
        return send(
            stage.at[0, k, 0, lo:hi], stage.at[0, k, 1 + i, lo:hi],
            xg_ss.at[p, i], xg_rs.at[p, i], x_peer[i],
        )

    def cg_copy(p, m):
        k, lo, hi = PARTS[p]
        r = slice(1, 4) if m else slice(0, 1)
        return send(
            stage.at[0, k, r, lo:hi], stage.at[1, k, r, lo:hi],
            cg_ss.at[p, m], cg_rs.at[p, m], other,
        )

    def spread(p):
        k, lo, hi = PARTS[p]
        if k == 0:
            for i in range(7):
                gather_copy(0, i).wait_recv()
        else:
            for j in range(lo, hi):
                gathered(j)
        for i in range(3):
            xg_copy(p, i).start()
        cg_copy(p, 0).start()

    def forward(p):
        for i in range(3):
            xg_copy(p, i).wait_recv()
        cg_copy(p, 1).start()

    def put(c, p, r):
        k, lo, hi = PARTS[p]
        half = core if c == 0 else 1 - core
        x = xs if r == 0 else (xs + NX - X_STEPS[r - 1]) % NX
        rows = pl.ds(pl.multiple_of(half * 64 + x * 16, 16), 16)
        for s in range(lo, hi):
            if k == 0:
                j = ys if s == 0 else (ys + 8 - RING[s - 1]) % 8
                out_ref[pl.ds(2 * j, 2), rows] = stage[c, 0, r, s]
            else:
                out_ref[16 + 2 * s : 18 + 2 * s, rows] = stage[c, 1, r, s]

    live = place[1] < LIVE[1]
    for j in range(LIVE[0]):
        first_total(0, j)
    for n in FAR_FIRST:
        first_copy(0, RING[n], n).start()
    for j in range(last):
        first_total(1, j)
    for n in FAR_FIRST:
        pl.when(early(n))(lambda n=n: first_copy(1, RING[n], n).start())
    first_total(1, last)
    pl.when(zs != last)(lambda: first_copy(1, last_step, 7).start())
    second_send(0)
    pl.when(live)(lambda: second_send(1))

    for c in halo + vol_halo:
        c.wait_send()
    for g in range(9):
        core_copies[g].wait_send()

    finish(0)
    gather(0)
    pl.when(live)(lambda: finish(1))
    pl.when(live)(lambda: gather(1))
    for g in range(9):
        for c in x_copies[g]:
            c.wait_send()
    for c in one_copies:
        c.wait_send()
    spread(0)
    spread(1)

    for n in range(7):
        first_copy(0, RING[n], n).wait_send()
    for n in range(7):
        pl.when(early(n))(lambda n=n: first_copy(1, RING[n], n).wait_send())
    pl.when(zs != last)(lambda: first_copy(1, last_step, 7).wait_send())

    def second_left(k):
        for i in range(7):
            second_copy(k, i).wait_send()

    second_left(0)
    pl.when(live)(lambda: second_left(1))
    def gather_left(k):
        for i in range(7):
            gather_copy(k, i).wait_send()

    gather_left(0)
    pl.when(live)(lambda: gather_left(1))
    put(0, 0, 0)
    put(0, 1, 0)
    spread(2)
    put(0, 2, 0)
    for p in range(3):
        forward(p)
        for r in range(1, 4):
            put(0, p, r)
        cg_copy(p, 0).wait_recv()
        put(1, p, 0)
    for p in range(3):
        for i in range(3):
            xg_copy(p, i).wait_send()
        cg_copy(p, 0).wait_send()
    for p in range(3):
        cg_copy(p, 1).wait_recv()
        for r in range(1, 4):
            put(1, p, r)
        cg_copy(p, 1).wait_send()


def widen(sums_ref, one_ref, two_ref, one, two, sem):
    outs = []
    for n in range(4):
        t = slice(7 * n, min(7 * n + 7, 27))
        two[t] = sums_ref[t].astype(F32)
        outs.append(pltpu.make_async_copy(two.at[t], two_ref.at[t], sem.at[n]))
        outs[n].start()
    rows = sums_ref[27].astype(F32)
    for n in range(27):
        one[n] = rows[4 * n : 4 * n + 4]
    outs.append(pltpu.make_async_copy(one, one_ref, sem.at[4]))
    outs[4].start()
    for c in outs:
        c.wait()


def body(volume, hidden_pre, grad_out, weight_two):
    hid = jnp.transpose(hidden_pre, (1, 2, 3, 0))
    grad = jnp.transpose(grad_out, (1, 2, 3, 0))
    weights = weight_two.reshape(9, 384, 128)
    dma = pltpu.SemaphoreType.DMA
    out = pl.pallas_call(
        kernel,
        out_shape=jax.ShapeDtypeStruct((TAPS, 128, 128), BF16),
        in_specs=[pl.BlockSpec(memory_space=pltpu.HBM)] * 4,
        out_specs=pl.BlockSpec(memory_space=pltpu.VMEM),
        scratch_shapes=[
            pltpu.VMEM((6, 10, 32, 128), BF16),
            pltpu.VMEM((9, 32, 256), BF16),
            pltpu.VMEM((4, 4, 8, 32), BF16),
            pltpu.VMEM((128, 128), F32),
            pltpu.VMEM((32, 256), F32),
            pltpu.VMEM((4, 8, 32, 128), BF16),
            pltpu.VMEM((9, 384, 128), BF16),
            pltpu.VMEM((384, 1024), BF16),
            pltpu.VMEM((TAPS, 128, 128), F32),
            pltpu.VMEM((27, 64, 128), F32),
            pltpu.VMEM((27, 64, 128), BF16),
            pltpu.VMEM((3, 27, 16, 128), BF16),
            pltpu.VMEM((7, 16, 128), F32),
            pltpu.VMEM((2, 8, 2, 16, 128), BF16),
            pltpu.VMEM((2, 8, 2, 16, 128), BF16),
            pltpu.VMEM((TAPS, 16, 128), F32),
            pltpu.VMEM((2, 8, 2, 16, 128), SUM),
            pltpu.VMEM((2, 2, 4, 8, 2, 16, 128), BF16),
            dma((4,)), dma((16,)), dma((16,)), dma((9,)), dma((9,)), dma((9, 3)), dma((9, 3)),
            dma((7,)), dma((7,)), dma((2, 8)), dma((2, 8)), dma((2, 7)), dma((2, 7)), dma((2, 7)), dma((2, 7)),
            dma((3, 3)), dma((3, 3)), dma((3, 2)), dma((3, 2)),
        ],
        compiler_params=pltpu.CompilerParams(
            collective_id=0, has_side_effects=True, vmem_limit_bytes=44 * 1024 * 1024
        ),
        name="conv_backward",
    )(*[pltpu.with_memory_space_constraint(x, pltpu.HBM) for x in (volume, hid, grad, weights)])
    one, two = pl.pallas_call(
        widen,
        out_shape=(
            jax.ShapeDtypeStruct((27, 4, 128), F32),
            jax.ShapeDtypeStruct((27, 128, 128), F32),
        ),
        in_specs=[pl.BlockSpec(memory_space=pltpu.VMEM)],
        out_specs=(pl.BlockSpec(memory_space=pl.ANY),) * 2,
        scratch_shapes=[
            pltpu.VMEM((27, 4, 128), F32),
            pltpu.VMEM((27, 128, 128), F32),
            dma((5,)),
        ],
        compiler_params=pltpu.CompilerParams(vmem_limit_bytes=8 * 1024 * 1024),
        name="widen",
    )(out)
    return (one.reshape(3, 3, 3, 4, 128), two.reshape(3, 3, 3, 128, 128))


def solution(mesh):
    in_specs = (
        P(None, "ha", "wa", None),
        P(None, "ha", "wa", None),
        P(None, "ha", "wa", None),
        P(),
    )
    return jax.shard_map(body, mesh=mesh, in_specs=in_specs, out_specs=(P(), P()), check_vma=False)
```

```python
import jax
import jax.numpy as jnp
from jax import lax
from jax.experimental import pallas as pl
from jax.experimental.pallas import tpu as pltpu
from jax.sharding import PartitionSpec as P

MESH = pl.DeviceIdType.MESH
F32 = jnp.float32
BF16 = jnp.bfloat16
NY, NZ, NX = 8, 8, 4
TAPS = 28
SIDES = [(a, b) for a in (-1, 0, 1) for b in (-1, 0, 1) if (a, b) != (0, 0)]
X_STEPS = (2, 1, 3)
RING = (1, 7, 2, 6, 3, 5, 4)
FAR_FIRST = (6, 5, 4, 3, 2, 1, 0)
LIVE = (8, 6)
SUMS = (F32, BF16)
PARTS = ((0, 0, 8), (1, 0, 5), (1, 5, 6))
ONE_STEPS = ((1, 2), (0, 2), (1, 1), (1, 3), (0, 1), (0, 3), (1, 0))


def span(side, size):
    if side == 0:
        return slice(0, size), slice(1, size + 1)
    if side == 1:
        return slice(size - 1, size), slice(0, 1)
    return slice(0, 1), slice(size + 1, size + 2)


def kernel(
    vol_ref, hid_ref, go_ref, w_ref, out_ref,
    ext, vols, vol_raw, vol_rows, vol_flat, hid, w, act_t, part, core_rx, x_tx, x_rx,
    one_rx, first_tx, first_rx, first_sum, second_0, second_1, stage,
    load_sem, halo_ss, halo_rs, core_ss, core_rs, x_ss, x_rs, o_ss, o_rs, f_ss, f_rs, s_ss, s_rs,
    g_ss, g_rs, xg_ss, xg_rs, cg_ss, cg_rs,
):
    ha = lax.axis_index("ha")
    wa = lax.axis_index("wa")
    ys, core = ha // 2, ha % 2
    zs, xs = wa // 4, wa % 4
    n_ha, n_wa = 2 * NY, NX * NZ

    def dev(y, c, z, x):
        return (y * 2 + c, z * NX + x)

    def near(side):
        return ((ha + side[0] + n_ha) % n_ha, (wa + side[1] + n_wa) % n_wa)

    other = dev(ys, 1 - core, zs, xs)
    x_peer = [dev(ys, core, zs, (xs + i) % NX) for i in X_STEPS]
    cross_peer = [dev(ys, 1 - core, zs, (xs + i) % NX) for i in X_STEPS]
    y_peer = [dev((ys + i) % NY, core, zs, xs) for i in RING]
    z_peer = [dev(ys, core, (zs + i) % NZ, xs) for i in RING]

    barrier = pltpu.get_barrier_semaphore()
    greet = [p[i] for i in FAR_FIRST for p in (z_peer, y_peer)]
    greet += cross_peer + x_peer + [near(s) for s in SIDES]
    for d in greet:
        pl.semaphore_signal(barrier, inc=1, device_id=d, device_id_type=MESH)

    loads = [
        pltpu.make_async_copy(vol_ref, vol_raw, load_sem.at[0]),
        pltpu.make_async_copy(hid_ref, hid, load_sem.at[1]),
        pltpu.make_async_copy(go_ref, ext.at[1:5, 1:9], load_sem.at[2]),
        pltpu.make_async_copy(w_ref, w, load_sem.at[3]),
    ]
    for c in loads:
        c.start()

    def send(src, dst, ss, rs, device):
        c = pltpu.make_async_remote_copy(
            src_ref=src, dst_ref=dst, send_sem=ss, recv_sem=rs,
            device_id=device, device_id_type=MESH,
        )
        return c

    halo, vol_halo = [], []
    for n, side in enumerate(SIDES):
        (sh, dh), (sw, dw) = span(side[0], 4), span(side[1], 8)
        slot = (1 - side[0]) * 3 + (1 - side[1])
        halo.append(send(go_ref.at[sh, sw], ext.at[dh, dw], halo_ss.at[n], halo_rs.at[n], near(side)))
        vol_halo.append(
            send(vols.at[4], vols.at[slot], halo_ss.at[8 + n], halo_rs.at[8 + n], near(side))
        )

    pl.semaphore_wait(barrier, len(greet))
    for c in halo:
        c.start()

    loads[0].wait()
    vol_rows[...] = jnp.zeros((128, 128), F32)
    vol_rows[:, 0:32] = vol_raw[...].astype(F32).reshape(128, 32)
    halves = []
    for half in range(2):
        lanes = jnp.zeros((16, 128), F32)
        for n in range(4):
            row = vol_rows[pl.ds(half * 4 + n, 16, stride=8), :]
            lanes = lanes + (pltpu.roll(row, 32 * n, 1) if n else row)
        halves.append(lanes)
    vol_flat[...] = jnp.zeros((32, 256), F32)
    for n in range(2):
        for c in range(4):
            for h in range(4):
                vol_flat[h * 8 + c : h * 8 + c + 1, 128 * n : 128 * n + 128] = halves[n][
                    c * 4 + h : c * 4 + h + 1
                ]
    vols[4] = vol_flat[...].astype(BF16)

    for c in vol_halo:
        c.start()

    loads[1].wait()
    depth = lax.broadcasted_iota(jnp.int32, (1024, 128), 0) % 32
    act = jnp.maximum(hid[...], 0).astype(F32).reshape(1024, 128)
    act_t[128:256, :] = act.astype(BF16).T
    lower = jnp.where(depth == 0, 0.0, pltpu.roll(act, 1, 0))
    act_t[0:128, :] = lower.astype(BF16).T
    upper = jnp.where(depth == 31, 0.0, pltpu.roll(act, 1023, 0))
    act_t[256:384, :] = upper.astype(BF16).T
    loads[2].wait()

    def window(g):
        kh, kw = g // 3, g % 3
        return ext[2 - kh : 6 - kh, 2 - kw : 10 - kw].reshape(1024, 128)

    def taps_of(g):
        return slice(3 * g, 3 * g + 3)

    their_half = pl.ds(pl.multiple_of((1 - core) * 64, 64), 64)
    own_half = pl.ds(pl.multiple_of(core * 64, 64), 64)
    own_in_half = pl.ds(pl.multiple_of(xs * 16, 16), 16)
    own_rows = pl.ds(pl.multiple_of(core * 64 + xs * 16, 16), 16)

    core_copies, x_copies = {}, {}

    def core_send(g):
        t = taps_of(g)
        c = send(part.at[t, their_half], core_rx.at[t], core_ss.at[g], core_rs.at[g], other)
        c.start()
        core_copies[g] = c

    def x_send(g):
        t = taps_of(g)
        core_copies[g].wait_recv()
        x_tx[t] = (part[t, own_half] + core_rx[t]).astype(BF16)
        x_copies[g] = []
        for i, step in enumerate(X_STEPS):
            rows = pl.ds(pl.multiple_of((xs + step) % NX * 16, 16), 16)
            c = send(x_tx.at[t, rows], x_rx.at[i, t], x_ss.at[g, i], x_rs.at[g, i], x_peer[i])
            c.start()
            x_copies[g].append(c)

    def grad_two(pair):
        right = jnp.concatenate([window(g) for g in pair], axis=1)
        terms = jnp.dot(act_t[...], right, preferred_element_type=F32)
        for n, g in enumerate(pair):
            part[taps_of(g)] = terms[:, 128 * n : 128 * n + 128].reshape(3, 128, 128)
            core_send(g)

    grad_two((4,))

    for c in halo:
        c.wait_recv()
    for edge, row in ((0, 0), (n_ha - 1, 5)):
        @pl.when(ha == edge)
        def _(row=row):
            ext[row : row + 1] = jnp.zeros((1, 10, 32, 128), BF16)

    for edge, col in ((0, 0), (n_wa - 1, 9)):
        @pl.when(wa == edge)
        def _(col=col):
            ext[:, col : col + 1] = jnp.zeros((6, 1, 32, 128), BF16)

    grad_two((0, 1))
    grad_two((2, 3))
    x_send(4)
    grad_two((5, 6))
    x_send(0)
    x_send(1)
    grad_two((7, 8))
    x_send(2)
    x_send(3)

    for c in vol_halo:
        c.wait_recv()
    for edge, first in ((0, 0), (n_ha - 1, 6)):
        @pl.when(ha == edge)
        def _(first=first):
            vols[first : first + 3] = jnp.zeros((3, 32, 256), BF16)

    for edge, first in ((0, 0), (n_wa - 1, 2)):
        @pl.when(wa == edge)
        def _(first=first):
            for n in (first, first + 3, first + 6):
                vols[n] = jnp.zeros((32, 256), BF16)

    def column(n):
        rows = [vols[n].astype(F32)[24:32], vols[3 + n].astype(F32), vols[6 + n].astype(F32)[0:8]]
        return jnp.concatenate(rows, axis=0)

    left, centre, right = column(0), column(1), column(2)
    lane = lax.broadcasted_iota(jnp.int32, (48, 256), 1)
    by_w = [
        jnp.where(lane < 32, pltpu.roll(left, 32, 1), pltpu.roll(centre, 32, 1)),
        centre,
        jnp.where(lane >= 224, pltpu.roll(right, 224, 1), pltpu.roll(centre, 224, 1)),
    ]
    blocks = []
    for field in by_w:
        blocks.append(jnp.where(lane % 32 == 0, 0.0, pltpu.roll(field, 1, 1)))
        blocks.append(field)
        blocks.append(jnp.where(lane % 32 == 31, 0.0, pltpu.roll(field, 255, 1)))

    loads[3].wait()
    one = [[jnp.zeros((8, 128), F32) for _ in range(3)] for _ in range(9)]
    depth_row = lax.broadcasted_iota(jnp.int32, (256, 128), 0) % 32
    weights = jnp.concatenate([w[g] for g in range(9)], axis=1)
    for h in range(4):
        cells = jnp.concatenate(
            [
                ext[h + 2 - g // 3, 2 - g % 3 : 10 - g % 3].reshape(256, 128)
                for g in range(9)
            ],
            axis=1,
        )
        pulled = lax.dot_general(
            cells, weights, (((1,), (1,)), ((), ())), preferred_element_type=F32
        )
        grad = (
            jnp.where(depth_row == 31, 0.0, pltpu.roll(pulled[:, 0:128], 255, 0))
            + pulled[:, 128:256]
            + jnp.where(depth_row == 0, 0.0, pltpu.roll(pulled[:, 256:384], 1, 0))
        )
        mask = hid[h].reshape(256, 128).astype(F32) > 0
        grad_hidden = jnp.where(mask, grad, 0.0).astype(BF16)
        fields = jnp.concatenate([block[8 * h : 8 * h + 24] for block in blocks], axis=0)
        terms = jnp.dot(fields.astype(BF16), grad_hidden, preferred_element_type=F32)
        for b in range(9):
            for kh in range(3):
                first = b * 24 + kh * 8
                one[b][kh] = one[b][kh] + terms[first : first + 8]
        if h == 0:
            x_send(5)
            x_send(6)
        if h == 1:
            x_send(7)
            x_send(8)
    part[27] = jnp.zeros((128, 128), F32)
    for b in range(9):
        for kh in range(3):
            first = (kh * 9 + b) * 4
            part[27, first : first + 4, :] = one[b][kh][0:4]
    one_copies = []
    for i, (c, step) in enumerate(ONE_STEPS):
        half = core if c == 0 else 1 - core
        rows = pl.ds(pl.multiple_of(half * 64 + (xs + step) % NX * 16, 16), 16)
        device = other if step == 0 else (cross_peer if c else x_peer)[X_STEPS.index(step)]
        one_copies.append(send(part.at[27, rows], one_rx.at[i], o_ss.at[i], o_rs.at[i], device))
        one_copies[i].start()

    place = (ys, zs)
    peers = (y_peer, z_peer)

    def first_copy(k, o, n):
        j = (place[k] + o) % 8
        target = dev(j, core, zs, xs) if k == 0 else dev(ys, core, j, xs)
        return send(first_tx.at[k, j], first_rx.at[k, o], f_ss.at[k, n], f_rs.at[k, o], target)

    seen = set()

    def first_total(k, j):
        lo = 16 * k + 2 * j
        hi = min(lo + 2, 27)
        for g in range(lo // 3, (hi - 1) // 3 + 1):
            if g not in seen:
                seen.add(g)
                for c in x_copies[g]:
                    c.wait_recv()
        t = slice(lo, hi)
        total = part[t, own_rows] + core_rx[t, own_in_half]
        for i in range(3):
            total = total + x_rx[i, t].astype(F32)
        first_sum[t] = total
        if hi == 27:
            one_total = part[27, own_rows]
            for i in range(7):
                one_copies[i].wait_recv()
                one_total = one_total + one_rx[i]
            first_sum[27] = one_total
        first_tx[k, j] = first_sum[lo : lo + 2].astype(BF16)

    last = LIVE[1] - 1
    last_step = (last + 8 - zs) % 8

    def early(n):
        return (zs + RING[n]) % 8 < last

    second = (second_0, second_1)

    def second_copy(k, i):
        at = second[k].at[place[1 - k]]
        return send(at, at, s_ss.at[k, i], s_rs.at[k, i], peers[1 - k][i])

    def second_send(k):
        for n in range(7):
            first_copy(k, RING[n], n).wait_recv()
        total = first_sum[pl.ds(16 * k + 2 * place[k], 2)]
        for n in range(7):
            total = total + first_rx[k, RING[n]].astype(F32)
        second[k][place[1 - k]] = total.astype(SUMS[k])
        for i in FAR_FIRST:
            second_copy(k, i).start()

    def gather_copy(k, i):
        if k == 0:
            return send(
                stage.at[0, 0, 0, 0], stage.at[0, 0, 0, 1 + i],
                g_ss.at[0, i], g_rs.at[0, i], y_peer[i],
            )
        at = stage.at[0, 1, 0, zs]
        return send(at, at, g_ss.at[1, i], g_rs.at[1, zs], z_peer[i])

    def gathered(j):
        at = stage.at[0, 1, 0, j]
        pl.when(zs != j)(lambda: send(at, at, g_ss.at[1, 0], g_rs.at[1, j], other).wait_recv())

    def finish(k):
        for i in range(7):
            second_copy(k, i).wait_recv()
        total = second[k][0].astype(F32)
        for s in range(1, 8):
            total = total + second[k][s].astype(F32)
        stage[0, k, 0, k * zs] = total.astype(BF16)

    def gather(k):
        for i in FAR_FIRST:
            gather_copy(k, i).start()

    def xg_copy(p, i):
        k, lo, hi = PARTS[p]
        return send(
            stage.at[0, k, 0, lo:hi], stage.at[0, k, 1 + i, lo:hi],
            xg_ss.at[p, i], xg_rs.at[p, i], x_peer[i],
        )

    def cg_copy(p, m):
        k, lo, hi = PARTS[p]
        r = slice(1, 4) if m else slice(0, 1)
        return send(
            stage.at[0, k, r, lo:hi], stage.at[1, k, r, lo:hi],
            cg_ss.at[p, m], cg_rs.at[p, m], other,
        )

    def spread(p):
        k, lo, hi = PARTS[p]
        if k == 0:
            for i in range(7):
                gather_copy(0, i).wait_recv()
        else:
            for j in range(lo, hi):
                gathered(j)
        for i in range(3):
            xg_copy(p, i).start()
        cg_copy(p, 0).start()

    def forward(p):
        for i in range(3):
            xg_copy(p, i).wait_recv()
        cg_copy(p, 1).start()

    def put(c, p, r):
        k, lo, hi = PARTS[p]
        half = core if c == 0 else 1 - core
        x = xs if r == 0 else (xs + NX - X_STEPS[r - 1]) % NX
        rows = pl.ds(pl.multiple_of(half * 64 + x * 16, 16), 16)
        for s in range(lo, hi):
            if k == 0:
                j = ys if s == 0 else (ys + 8 - RING[s - 1]) % 8
                out_ref[pl.ds(2 * j, 2), rows] = stage[c, 0, r, s]
            else:
                out_ref[16 + 2 * s : 18 + 2 * s, rows] = stage[c, 1, r, s]

    live = place[1] < LIVE[1]
    for j in range(LIVE[0]):
        first_total(0, j)
    for n in FAR_FIRST:
        first_copy(0, RING[n], n).start()
    for j in range(last):
        first_total(1, j)
    for n in FAR_FIRST:
        pl.when(early(n))(lambda n=n: first_copy(1, RING[n], n).start())
    first_total(1, last)
    pl.when(zs != last)(lambda: first_copy(1, last_step, 7).start())
    second_send(0)
    pl.when(live)(lambda: second_send(1))

    for c in halo + vol_halo:
        c.wait_send()
    for g in range(9):
        core_copies[g].wait_send()

    finish(0)
    gather(0)
    pl.when(live)(lambda: finish(1))
    pl.when(live)(lambda: gather(1))
    for g in range(9):
        for c in x_copies[g]:
            c.wait_send()
    for c in one_copies:
        c.wait_send()
    spread(0)
    spread(1)

    for n in range(7):
        first_copy(0, RING[n], n).wait_send()
    for n in range(7):
        pl.when(early(n))(lambda n=n: first_copy(1, RING[n], n).wait_send())
    pl.when(zs != last)(lambda: first_copy(1, last_step, 7).wait_send())

    def second_left(k):
        for i in range(7):
            second_copy(k, i).wait_send()

    second_left(0)
    pl.when(live)(lambda: second_left(1))
    def gather_left(k):
        for i in range(7):
            gather_copy(k, i).wait_send()

    gather_left(0)
    pl.when(live)(lambda: gather_left(1))
    put(0, 0, 0)
    put(0, 1, 0)
    spread(2)
    put(0, 2, 0)
    for p in range(3):
        forward(p)
        for r in range(1, 4):
            put(0, p, r)
        cg_copy(p, 0).wait_recv()
        put(1, p, 0)
    for p in range(3):
        for i in range(3):
            xg_copy(p, i).wait_send()
        cg_copy(p, 0).wait_send()
    for p in range(3):
        cg_copy(p, 1).wait_recv()
        for r in range(1, 4):
            put(1, p, r)
        cg_copy(p, 1).wait_send()


def widen(sums_ref, one_ref, two_ref, one, two, sem):
    outs = []
    for n in range(4):
        t = slice(7 * n, min(7 * n + 7, 27))
        two[t] = sums_ref[t].astype(F32)
        outs.append(pltpu.make_async_copy(two.at[t], two_ref.at[t], sem.at[n]))
        outs[n].start()
    rows = sums_ref[27].astype(F32)
    for n in range(27):
        one[n] = rows[4 * n : 4 * n + 4]
    outs.append(pltpu.make_async_copy(one, one_ref, sem.at[4]))
    outs[4].start()
    for c in outs:
        c.wait()


def body(volume, hidden_pre, grad_out, weight_two):
    hid = jnp.transpose(hidden_pre, (1, 2, 3, 0))
    grad = jnp.transpose(grad_out, (1, 2, 3, 0))
    weights = weight_two.reshape(9, 384, 128)
    dma = pltpu.SemaphoreType.DMA
    out = pl.pallas_call(
        kernel,
        out_shape=jax.ShapeDtypeStruct((TAPS, 128, 128), BF16),
        in_specs=[pl.BlockSpec(memory_space=pltpu.HBM)] * 4,
        out_specs=pl.BlockSpec(memory_space=pltpu.VMEM),
        scratch_shapes=[
            pltpu.VMEM((6, 10, 32, 128), BF16),
            pltpu.VMEM((9, 32, 256), BF16),
            pltpu.VMEM((4, 4, 8, 32), BF16),
            pltpu.VMEM((128, 128), F32),
            pltpu.VMEM((32, 256), F32),
            pltpu.VMEM((4, 8, 32, 128), BF16),
            pltpu.VMEM((9, 384, 128), BF16),
            pltpu.VMEM((384, 1024), BF16),
            pltpu.VMEM((TAPS, 128, 128), F32),
            pltpu.VMEM((27, 64, 128), F32),
            pltpu.VMEM((27, 64, 128), BF16),
            pltpu.VMEM((3, 27, 16, 128), BF16),
            pltpu.VMEM((7, 16, 128), F32),
            pltpu.VMEM((2, 8, 2, 16, 128), BF16),
            pltpu.VMEM((2, 8, 2, 16, 128), BF16),
            pltpu.VMEM((TAPS, 16, 128), F32),
            pltpu.VMEM((8, 2, 16, 128), SUMS[0]),
            pltpu.VMEM((8, 2, 16, 128), SUMS[1]),
            pltpu.VMEM((2, 2, 4, 8, 2, 16, 128), BF16),
            dma((4,)), dma((16,)), dma((16,)), dma((9,)), dma((9,)), dma((9, 3)), dma((9, 3)),
            dma((7,)), dma((7,)), dma((2, 8)), dma((2, 8)), dma((2, 7)), dma((2, 7)), dma((2, 7)), dma((2, 7)),
            dma((3, 3)), dma((3, 3)), dma((3, 2)), dma((3, 2)),
        ],
        compiler_params=pltpu.CompilerParams(
            collective_id=0, has_side_effects=True, vmem_limit_bytes=44 * 1024 * 1024
        ),
        name="conv_backward",
    )(*[pltpu.with_memory_space_constraint(x, pltpu.HBM) for x in (volume, hid, grad, weights)])
    one, two = pl.pallas_call(
        widen,
        out_shape=(
            jax.ShapeDtypeStruct((27, 4, 128), F32),
            jax.ShapeDtypeStruct((27, 128, 128), F32),
        ),
        in_specs=[pl.BlockSpec(memory_space=pltpu.VMEM)],
        out_specs=(pl.BlockSpec(memory_space=pl.ANY),) * 2,
        scratch_shapes=[
            pltpu.VMEM((27, 4, 128), F32),
            pltpu.VMEM((27, 128, 128), F32),
            dma((5,)),
        ],
        compiler_params=pltpu.CompilerParams(vmem_limit_bytes=8 * 1024 * 1024),
        name="widen",
    )(out)
    return (one.reshape(3, 3, 3, 4, 128), two.reshape(3, 3, 3, 128, 128))


def solution(mesh):
    in_specs = (
        P(None, "ha", "wa", None),
        P(None, "ha", "wa", None),
        P(None, "ha", "wa", None),
        P(),
    )
    return jax.shard_map(body, mesh=mesh, in_specs=in_specs, out_specs=(P(), P()), check_vma=False)
```
